256 devices in a mesh: rep: 4 (over z_hi, core), fsdp: 64 (over z_lo, y, x).
Axes of the slice: x: 4, y: 4, z: 8 (z_hi: 2, z_lo: 4; z = z_hi * 4 + z_lo), core: 2. Of those that a mesh axis runs over, the one named last changes fastest.
Arguments:
- tokens: bfloat16 [81920, 8192], P(('rep', 'fsdp')), may hold values from -24 to 24
- cotangent: bfloat16 [81920, 512], P(('rep', 'fsdp')), may hold values from -0.5 to 0.5
- weight: bfloat16 [4, 8192, 512], P('rep', 'fsdp'), may hold values from -0.25 to 0.25
- norm_gain: bfloat16 [4, 8192], P('rep', 'fsdp'), may hold values from 0.099609375 to 1.8984375
- fragment_index: int32 [1], replicated, may hold values from 0 to 4095
- assignment: int32 [8], replicated, may hold values from 0 to 3, as said below
- outer_params: float32 [8, 524288], P(None, 'fsdp'), may hold values from -6 to 6
- momentum: float32 [8, 524288], P(None, 'fsdp'), may hold values from -3 to 3
- local_params: bfloat16 [4, 8, 524288], P('rep', None, 'fsdp'), may hold values from -6 to 6
Outputs:
- values: bfloat16 [81920, 512], P(('rep', 'fsdp'))
- token_grad: bfloat16 [81920, 8192], P(('rep', 'fsdp'))
- weight_grad: float32 [4, 8192, 512], P('rep', 'fsdp')
- gain_grad: float32 [4, 8192], P('rep', 'fsdp')
- outer_new: float32 [8, 524288], P(None, 'fsdp')
- momentum_new: float32 [8, 524288], P(None, 'fsdp')
- local_new: bfloat16 [4, 8, 524288], P('rep', None, 'fsdp')
The draws below stay inside these ranges and needn't reach their ends.
Inputs may be any that keep to these rules, and one draw needn't show every extreme that they name: `assignment`: each of the 4 fragment numbers is assigned to exactly 2 layers.
All inputs are finite; a program needn't handle non-finite values.
Results may differ from the reference program's by a relative error of at most 0.012.
Values may be sent and summed in bfloat16 or wider, within the bound.
No kernel may reach another device: no remote copies, remote signals or barrier semaphores. Data moves between devices by JAX's collectives and lax.ppermute only.
A program may use at most 192 MiB of HBM per device.

```python
import jax
import jax.numpy as jnp
from jax import lax

D = 8192
KV = 512
TOK_DEV = 320
FLAYERS = 8
NFRAG = 4
FRAG = 524288
TOKENS = 81920
N_REP = 4
N_FSDP = 64


def draw_assignment(key, part):
    key = jax.random.fold_in(key, 7)
    order = jax.random.permutation(key, FLAYERS)
    return (order % NFRAG).astype(jnp.int32)


def raised(values, own_key, source, target, parts, factor):
    def block_of(position):
        return (jnp.arange(values.shape[position]) // (values.shape[position] // parts)).reshape((-1,) + (1,) * (values.ndim - 1 - position))

    one_side = jax.random.permutation(own_key, parts)[block_of(target)]
    far = (block_of(target) + parts // 2) % parts
    return jnp.where((block_of(source) == one_side) | (block_of(source) == far), factor * values, values)


def block_scale(rng, shape, cuts, smallest, largest):
    loudness = 1.0
    for axis_at, parts in cuts:
        steps = jax.random.uniform(jax.random.fold_in(jax.random.fold_in(rng, 6), axis_at), (parts,), jnp.float32, smallest / len(cuts), largest / len(cuts))
        loudness = loudness * jnp.repeat(jnp.exp(steps), shape[axis_at] // parts).reshape((-1,) + (1,) * (len(shape) - 1 - axis_at))
    return loudness


def gaussian(key, dims, width, most, cuts=(), dtype=jnp.bfloat16):
    level = block_scale(key, dims, cuts, -0.22, 0.18) if cuts else 1.0
    result = jax.random.normal(key, dims, jnp.float32) * width * level
    return jnp.minimum(jnp.maximum(result, -most), most).astype(dtype)


def noise_with(rng, extent, deviation, limit, pieces, heavy, held_as=jnp.bfloat16):
    result = deviation * jax.random.normal(rng, extent, jnp.float32)
    if pieces:
        result = result * block_scale(rng, extent, pieces, -0.22, 0.18)
    return jnp.clip(raised(result, jax.random.fold_in(rng, 3), *heavy), -limit, limit).astype(held_as)


def setup_inputs(seed: int = 0) -> dict:
    keys = jax.random.split(jax.random.key(seed), 10)
    tokens = noise_with(keys[0], (TOKENS, D), 1.0, 24.0, ((0, 256),), (0, 1, 256, 6.0))
    cotangent = gaussian(keys[1], (TOKENS, KV), 0.0625, 0.5, ((0, 256),))
    weight = gaussian(keys[2], (N_REP, D, KV), KV ** -0.5, 0.25, ((0, 4), (1, 64)))
    norm_gain = jnp.clip(1.0 + 0.18 * jax.random.normal(keys[3], (N_REP, D), jnp.float32), 0.099609375, 1.8984375).astype(jnp.bfloat16)
    fragment_index = jax.random.randint(keys[4], (1,), 0, 4096).astype(jnp.int32)
    assignment = draw_assignment(jax.random.fold_in(keys[9], 71), 0)
    outer_params = gaussian(keys[6], (FLAYERS, FRAG), 1.0, 6.0, ((1, 64),), jnp.float32)
    momentum = gaussian(keys[7], (FLAYERS, FRAG), 0.5, 3.0, ((1, 64),), jnp.float32)
    local_params = gaussian(keys[8], (N_REP, FLAYERS, FRAG), 1.0, 6.0, ((0, 4), (2, 64)))
    return {"tokens": tokens, "cotangent": cotangent, "weight": weight, "norm_gain": norm_gain, "fragment_index": fragment_index, "assignment": assignment, "outer_params": outer_params, "momentum": momentum, "local_params": local_params}


epsilon = 1e-05
outer_rate = 0.7
nesterov = 0.9
mixing = 0.5

def replica_pass(items):
    tokens, cotangent, weight, norm_gain = items
    xfloat = tokens.astype(jnp.float32)
    scales = lax.rsqrt(lax.optimization_barrier(jnp.mean(xfloat * xfloat, axis=-1, keepdims=True)) + epsilon)
    gain_full = norm_gain.astype(jnp.float32)
    normed = (xfloat * scales * gain_full).astype(jnp.bfloat16)
    values = jnp.dot(normed, weight, preferred_element_type=jnp.float32).astype(jnp.bfloat16)
    upstream = jnp.dot(cotangent, weight.T, preferred_element_type=jnp.float32)
    weighted = upstream * gain_full
    token_grad = (scales * weighted - xfloat * (scales * scales * scales) * lax.optimization_barrier(jnp.mean(weighted * xfloat, axis=-1, keepdims=True))).astype(jnp.bfloat16)
    weight_grad = jnp.dot(normed.T, cotangent, preferred_element_type=jnp.float32)
    gain_grad = lax.optimization_barrier(jnp.sum(upstream * xfloat * scales, axis=0))
    return (values, token_grad, weight_grad, gain_grad)

def reference(tokens, cotangent, weight, norm_gain, fragment_index, assignment, outer_params, momentum, local_params):
    rep_rows = TOK_DEV * N_FSDP
    stacked = (tokens.reshape(N_REP, rep_rows, D), cotangent.reshape(N_REP, rep_rows, KV), weight, norm_gain)
    values, token_grad, weight_grad, gain_grad = lax.map(replica_pass, stacked)
    values = values.reshape(N_REP * rep_rows, KV)
    token_grad = token_grad.reshape(N_REP * rep_rows, D)
    current = jnp.remainder(fragment_index[0], NFRAG).astype(jnp.int32)
    selected = (assignment == current)[:, None]
    local_float = local_params.astype(jnp.float32)
    outer_delta = lax.optimization_barrier(jnp.sum(outer_params[None] - local_float, axis=0)) / N_REP
    outer_delta = jnp.where(selected, outer_delta, jnp.float32(0.0))
    momentum_new = jnp.where(selected, nesterov * momentum + outer_delta, momentum)
    outer_new = jnp.where(selected, outer_params - outer_rate * (outer_delta + nesterov * momentum_new), outer_params)
    blended = (mixing * local_float + (1.0 - mixing) * outer_new[None]).astype(jnp.bfloat16)
    local_new = jnp.where(selected[None], blended, local_params)
    return (values, token_grad, weight_grad, gain_grad, outer_new, momentum_new, local_new)
```

```python
import jax
import jax.numpy as jnp
from jax import lax
from jax.sharding import PartitionSpec as P

NFRAG = 4
SIDE = 4
ROWS = 128
KV = 512
HALF = KV // 2

epsilon = 1e-05
outer_rate = 0.7
nesterov = 0.9
mixing = 0.5


def flat(z, y, x):
    return (z * SIDE + y) * SIDE + x


def ring(axis, step):
    pairs = []
    for z in range(SIDE):
        for y in range(SIDE):
            for x in range(SIDE):
                to = [z, y, x]
                to[axis] = (to[axis] + step) % SIDE
                pairs.append((flat(z, y, x), flat(*to)))
    return pairs


def lines(axis):
    groups = []
    for a in range(SIDE):
        for b in range(SIDE):
            group = []
            for c in range(SIDE):
                at = [a, b]
                at.insert(axis, c)
                group.append(flat(*at))
            groups.append(group)
    return groups


def hop(value, axis, step):
    return lax.ppermute(value, "fsdp", ring(axis, step))


def gather_small(own, axis, place):
    parts = [own] + [hop(own, axis, -step) for step in (1, 2, 3)]
    stacked = jnp.stack(parts)
    order = (jnp.arange(SIDE) - place) % SIDE
    return jnp.take(stacked, order, axis=0)


def gather_large(own, axis, place):
    a, b = own[:2], own[2:]
    prev_a, next_b = hop(a, axis, 1), hop(b, axis, -1)
    prev_b, next_a = hop(b, axis, 1), hop(a, axis, -1)
    far_a, far_b = hop(prev_a, axis, 1), hop(next_b, axis, -1)
    return [
        (place, a, b),
        ((place + 3) % SIDE, prev_a, prev_b),
        ((place + 1) % SIDE, next_a, next_b),
        ((place + 2) % SIDE, far_a, far_b),
    ]


def add(left, right):
    return (left.astype(jnp.float32) + right.astype(jnp.float32)).astype(jnp.bfloat16)


def reduce_large(pick, axis, place):
    far, after, before, own = (pick((place + d) % SIDE) for d in (2, 1, 3, 0))
    far_a, far_b = hop(far[:2], axis, 1), hop(far[2:], axis, -1)
    got_b, sent_a = hop(after[2:], axis, 1), hop(before[:2], axis, -1)
    got_a = hop(add(after[:2], far_a), axis, 1)
    sent_b = hop(add(before[2:], far_b), axis, -1)
    def total(one, two, three):
        return (one.astype(jnp.float32) + two.astype(jnp.float32) + three.astype(jnp.float32)).astype(jnp.bfloat16)
    return jnp.concatenate([total(own[:2], got_a, sent_a), total(own[2:], got_b, sent_b)])


def reduce_small(term, axis, place):
    total = lax.dynamic_index_in_dim(term, place, 0, False).astype(jnp.float32)
    for step in (1, 2, 3):
        sent = lax.dynamic_index_in_dim(term, (place + step) % SIDE, 0, False)
        total = total + hop(sent, axis, step).astype(jnp.float32)
    return total


def shards(
    tokens,
    cotangent,
    weight,
    norm_gain,
    fragment_index,
    assignment,
    outer_params,
    momentum,
    local_params,
):
    at = lax.axis_index("fsdp")
    y, x = (at // SIDE) % SIDE, at % SIDE
    gain = norm_gain[0].astype(jnp.float32)[:, None]
    owned = (weight[0].astype(jnp.float32) * gain).astype(jnp.bfloat16)

    row = gather_small(owned[:, :HALF], 2, x)
    column = gather_small(owned[:, HALF:], 1, y)
    plane = lax.all_gather(row, "fsdp", axis_index_groups=lines(0))
    other = lax.all_gather(column, "fsdp", axis_index_groups=lines(0))

    xfloat = tokens.astype(jnp.float32)
    scales = lax.rsqrt(jnp.mean(xfloat * xfloat, axis=-1, keepdims=True) + epsilon)
    scaled = (cotangent.astype(jnp.float32) * scales).astype(jnp.bfloat16)

    def term(half):
        return lax.dot_general(
            tokens, half, (((0,), (0,)), ((), ())), preferred_element_type=jnp.float32
        ).astype(jnp.bfloat16).reshape(SIDE, SIDE, SIDE, ROWS, HALF)

    left, right = term(scaled[:, :HALF]), term(scaled[:, HALF:])
    left = reduce_large(lambda i: lax.dynamic_index_in_dim(left, i, 1, False), 1, y)
    right = reduce_large(lambda i: lax.dynamic_index_in_dim(right, i, 2, False), 2, x)
    left = lax.psum_scatter(left, "fsdp", scatter_dimension=0, axis_index_groups=lines(0))
    right = lax.psum_scatter(right, "fsdp", scatter_dimension=0, axis_index_groups=lines(0))

    first = jnp.zeros((SIDE, SIDE, SIDE, ROWS, HALF), jnp.bfloat16)
    second = first
    for position, a, b in gather_large(plane, 1, y):
        whole = jnp.concatenate([a, b])
        first = lax.dynamic_update_index_in_dim(first, whole, position, 1)
    for position, a, b in gather_large(other, 2, x):
        whole = jnp.concatenate([a, b])
        second = lax.dynamic_update_index_in_dim(second, whole, position, 2)
    first = first.reshape(-1, HALF)
    second = second.reshape(-1, HALF)

    product = jnp.concatenate(
        [jnp.dot(tokens, part, preferred_element_type=jnp.float32) for part in (first, second)], axis=1
    )
    values = (product * scales).astype(jnp.bfloat16)
    mean = jnp.sum(product * cotangent.astype(jnp.float32), axis=-1, keepdims=True) / tokens.shape[1]
    by_columns = (((1,), (1,)), ((), ()))
    weighted = lax.dot_general(
        cotangent[:, :HALF], first, by_columns, preferred_element_type=jnp.float32
    ) + lax.dot_general(cotangent[:, HALF:], second, by_columns, preferred_element_type=jnp.float32)
    token_grad = (scales * weighted - xfloat * (scales * scales * scales * mean)).astype(jnp.bfloat16)

    summed = jnp.concatenate([reduce_small(left, 2, x), reduce_small(right, 1, y)], axis=1)
    weight_grad = (summed * gain)[None]
    gain_grad = jnp.sum(summed * weight[0].astype(jnp.float32), axis=1)[None]

    current = jnp.remainder(fragment_index[0], NFRAG)
    selected = assignment == current
    layers = assignment.shape[0]
    one = jnp.argmax(selected)
    two = layers - 1 - jnp.argmax(selected[::-1])
    local = local_params[0]
    chosen = jnp.stack([lax.dynamic_index_in_dim(local, i, 0, False) for i in (one, two)])
    replicas = lax.axis_size("rep")
    total = jnp.sum(
        lax.all_gather(chosen, "rep").astype(jnp.float32), axis=0
    )
    spread = jnp.where(
        (jnp.arange(layers) == one)[:, None], total[0][None], total[1][None]
    )
    outer_delta = (replicas * outer_params - spread) / replicas
    momentum_new = jnp.where(selected[:, None], nesterov * momentum + outer_delta, momentum)
    outer_new = jnp.where(
        selected[:, None],
        outer_params - outer_rate * (outer_delta + nesterov * momentum_new),
        outer_params,
    )
    blended = (mixing * local.astype(jnp.float32) + (1.0 - mixing) * outer_new).astype(jnp.bfloat16)
    local_new = jnp.where(selected[:, None], blended, local)[None]
    return (values, token_grad, weight_grad, gain_grad, outer_new, momentum_new, local_new)


def solution(mesh):
    in_specs = (
        P(("rep", "fsdp"), None),
        P(("rep", "fsdp"), None),
        P("rep", "fsdp", None),
        P("rep", "fsdp"),
        P(),
        P(),
        P(None, "fsdp"),
        P(None, "fsdp"),
        P("rep", None, "fsdp"),
    )
    out_specs = (
        P(("rep", "fsdp"), None),
        P(("rep", "fsdp"), None),
        P("rep", "fsdp", None),
        P("rep", "fsdp"),
        P(None, "fsdp"),
        P(None, "fsdp"),
        P("rep", None, "fsdp"),
    )
    return jax.shard_map(shards, mesh=mesh, in_specs=in_specs, out_specs=out_specs, check_vma=False)
```

```python
import jax
import jax.numpy as jnp
from jax import lax
from jax.experimental import pallas as pl
from jax.experimental.pallas import tpu as pltpu
from jax.sharding import PartitionSpec as P

NFRAG = 4
SIDE = 4
ROWS = 128
KV = 512
HALF = KV // 2
WIDE = SIDE * ROWS
VMEM_LIMIT = 56 * 1024 * 1024

epsilon = 1e-05
outer_rate = 0.7
nesterov = 0.9
mixing = 0.5


def flat(z, y, x):
    return (z * SIDE + y) * SIDE + x


def ring(axis, step):
    pairs = []
    for z in range(SIDE):
        for y in range(SIDE):
            for x in range(SIDE):
                to = [z, y, x]
                to[axis] = (to[axis] + step) % SIDE
                pairs.append((flat(z, y, x), flat(*to)))
    return pairs


def lines(axis):
    groups = []
    for a in range(SIDE):
        for b in range(SIDE):
            group = []
            for c in range(SIDE):
                at = [a, b]
                at.insert(axis, c)
                group.append(flat(*at))
            groups.append(group)
    return groups


def hop(value, axis, step):
    return lax.ppermute(value, "fsdp", ring(axis, step))


def gather_small(own, axis, place):
    parts = [own] + [hop(own, axis, -step) for step in (1, 2, 3)]
    return lax.dynamic_slice_in_dim(jnp.stack(parts + parts), (SIDE - place) % SIDE, SIDE)


def gather_large(a, b, axis):
    prev_a, next_b = hop(a, axis, 1), hop(b, axis, -1)
    prev_b, next_a = hop(b, axis, 1), hop(a, axis, -1)
    far_a, far_b = hop(prev_a, axis, 1), hop(next_b, axis, -1)
    return [next_a, next_b, far_a, far_b, prev_a, prev_b]


def total(*terms):
    return sum(t.astype(jnp.float32) for t in terms).astype(jnp.bfloat16)


def reduce_large(pieces, axis):
    own_a, own_b, after_a, after_b, far_a, far_b, before_a, before_b = pieces
    far_a, far_b = hop(far_a, axis, 1), hop(far_b, axis, -1)
    got_b, sent_a = hop(after_b, axis, 1), hop(before_a, axis, -1)
    got_a = hop(total(after_a, far_a), axis, 1)
    sent_b = hop(total(before_b, far_b), axis, -1)
    return total(own_a, got_a, sent_a), total(own_b, got_b, sent_b)


def reduce_small(term, axis, place):
    result = lax.dynamic_index_in_dim(term, place, 0, False).astype(jnp.float32)
    for step in (1, 2, 3):
        sent = lax.dynamic_index_in_dim(term, (place + step) % SIDE, 0, False)
        result = result + hop(sent, axis, step).astype(jnp.float32)
    return result


def terms_kernel(at, x_ref, cot_ref, scale_ref, *rest):
    outs, (turned, block) = rest[:16], rest[16:]
    width = x_ref.shape[1]
    squares = jnp.zeros((x_ref.shape[0], ROWS), jnp.float32)
    for j in range(width // ROWS):
        part = x_ref[:, j * ROWS : (j + 1) * ROWS].astype(jnp.float32)
        squares = squares + part * part
    mean = jnp.sum(squares, axis=-1, keepdims=True) / width
    scale = lax.rsqrt(mean + epsilon)
    scale_ref[...] = scale
    scaled = cot_ref[...].astype(jnp.float32) * scale
    turned[...] = scaled.T.astype(jnp.bfloat16)
    for z in range(SIDE):
        for dy in range(SIDE):
            y = lax.rem(at[0] + dy, SIDE)
            start = pl.multiple_of((z * SIDE + y) * WIDE, WIDE)
            product = jnp.dot(
                turned[...], x_ref[:, pl.ds(start, WIDE)], preferred_element_type=jnp.float32
            )
            out = outs[2 * dy + z // 2]
            for x in range(SIDE):
                out[z % 2, x] = product[:HALF, x * ROWS : (x + 1) * ROWS].astype(jnp.bfloat16)
            block[...] = product[HALF:].astype(jnp.bfloat16)
            for dx in range(SIDE):
                x = lax.rem(at[1] + dx, SIDE)
                out = outs[8 + 2 * dx + z // 2]
                out[z % 2, y] = block[:, pl.ds(pl.multiple_of(x * ROWS, ROWS), ROWS)]


def make_terms(at, tokens, cotangent):
    rows, width = tokens.shape
    piece = jax.ShapeDtypeStruct((2, SIDE, HALF, ROWS), jnp.bfloat16)
    vmem = pl.BlockSpec(memory_space=pltpu.VMEM)
    scale, *pieces = pl.pallas_call(
        terms_kernel,
        out_shape=[jax.ShapeDtypeStruct((rows, 1), jnp.float32)] + [piece] * 16,
        in_specs=[pl.BlockSpec(memory_space=pltpu.SMEM), vmem, vmem],
        out_specs=[vmem] * 17,
        scratch_shapes=[pltpu.VMEM((KV, rows), jnp.bfloat16), pltpu.VMEM((HALF, WIDE), jnp.bfloat16)],
        compiler_params=pltpu.CompilerParams(vmem_limit_bytes=VMEM_LIMIT),
        cost_estimate=pl.CostEstimate(
            flops=2 * rows * width * KV, bytes_accessed=2 * width * (rows + KV), transcendentals=rows
        ),
    )(at, tokens, cotangent)
    return scale, pieces[:8], pieces[8:]


def project_kernel(at, x_ref, cot_ref, scale_ref, plane, *rest):
    pieces, (values_ref, grad_ref), (first, second) = rest[:12], rest[12:14], rest[14:]
    width = x_ref.shape[1]
    for z in range(SIDE):
        for d in range(SIDE):
            y, x = lax.rem(at[0] + d, SIDE), lax.rem(at[1] + d, SIDE)
            for j in range(SIDE):
                if d == 0:
                    first[z, y, j] = plane[z, j]
                    second[z, j, x] = plane[z, SIDE + j]
                else:
                    first[z, y, j] = pieces[2 * d - 2 + z // 2][z % 2, j]
                    second[z, j, x] = pieces[6 + 2 * d - 2 + z // 2][z % 2, j]
    scale = scale_ref[...]
    depth = SIDE * WIDE
    mean = jnp.zeros_like(scale)
    for h, matrix in enumerate((first, second)):
        columns = slice(h * HALF, (h + 1) * HALF)
        product = jnp.zeros((x_ref.shape[0], HALF), jnp.float32)
        for z in range(SIDE):
            product = product + jnp.dot(
                x_ref[:, z * depth : (z + 1) * depth],
                matrix[z].reshape(depth, HALF),
                preferred_element_type=jnp.float32,
            )
        values_ref[:, columns] = (product * scale).astype(jnp.bfloat16)
        mean = mean + jnp.sum(product * cot_ref[:, columns].astype(jnp.float32), axis=-1, keepdims=True)
    slope = scale * scale * scale * (mean / width)
    by_columns = (((1,), (1,)), ((), ()))
    for z in range(SIDE):
        for y in range(SIDE):
            weighted = lax.dot_general(
                cot_ref[:, :HALF], first[z, y].reshape(WIDE, HALF), by_columns, preferred_element_type=jnp.float32
            ) + lax.dot_general(
                cot_ref[:, HALF:], second[z, y].reshape(WIDE, HALF), by_columns, preferred_element_type=jnp.float32
            )
            start = (z * SIDE + y) * WIDE
            columns = slice(start, start + WIDE)
            grad_ref[:, columns] = (
                scale * weighted - x_ref[:, columns].astype(jnp.float32) * slope
            ).astype(jnp.bfloat16)


def project(at, tokens, cotangent, scale, plane, pieces):
    rows, width = tokens.shape
    vmem = pl.BlockSpec(memory_space=pltpu.VMEM)
    whole = pltpu.VMEM((SIDE, SIDE, SIDE, ROWS, HALF), jnp.bfloat16)
    return pl.pallas_call(
        project_kernel,
        out_shape=[
            jax.ShapeDtypeStruct((rows, KV), jnp.bfloat16),
            jax.ShapeDtypeStruct((rows, width), jnp.bfloat16),
        ],
        in_specs=[pl.BlockSpec(memory_space=pltpu.SMEM)] + [vmem] * 16,
        out_specs=[vmem] * 2,
        scratch_shapes=[whole, whole],
        compiler_params=pltpu.CompilerParams(vmem_limit_bytes=VMEM_LIMIT),
        cost_estimate=pl.CostEstimate(
            flops=4 * rows * width * KV, bytes_accessed=2 * width * (2 * rows + KV), transcendentals=0
        ),
    )(at, tokens, cotangent, scale, plane, *pieces)


def outer_step(fragment_index, assignment, outer_params, momentum, local):
    layers = assignment.shape[0]
    selected = assignment == jnp.remainder(fragment_index[0], NFRAG)
    one = jnp.argmax(selected)
    two = layers - 1 - jnp.argmax(selected[::-1])
    chosen = jnp.stack([lax.dynamic_index_in_dim(local, i, 0, False) for i in (one, two)])
    replicas = lax.axis_size("rep")
    chip = jnp.stack([chosen, lax.ppermute(chosen, "rep", [(r, r ^ 1) for r in range(replicas)])])
    away = lax.ppermute(chip, "rep", [(r, r ^ 2) for r in range(replicas)])
    summed = jnp.sum(chip.astype(jnp.float32) + away.astype(jnp.float32), axis=0)
    spread = jnp.where((jnp.arange(layers) == one)[:, None], summed[0][None], summed[1][None])
    outer_delta = (replicas * outer_params - spread) / replicas
    momentum_new = jnp.where(selected[:, None], nesterov * momentum + outer_delta, momentum)
    outer_new = jnp.where(
        selected[:, None],
        outer_params - outer_rate * (outer_delta + nesterov * momentum_new),
        outer_params,
    )
    blended = (mixing * local.astype(jnp.float32) + (1.0 - mixing) * outer_new).astype(jnp.bfloat16)
    return outer_new, momentum_new, jnp.where(selected[:, None], blended, local)


def shards(
    tokens,
    cotangent,
    weight,
    norm_gain,
    fragment_index,
    assignment,
    outer_params,
    momentum,
    local_params,
):
    index = lax.axis_index("fsdp")
    y, x = (index // SIDE) % SIDE, index % SIDE
    at = jnp.stack([y, x]).astype(jnp.int32)
    gain = norm_gain[0].astype(jnp.float32)
    matrix = weight[0].astype(jnp.float32)
    owned = (matrix * gain[:, None]).astype(jnp.bfloat16)

    row = gather_small(owned[:, :HALF], 2, x)
    column = gather_small(owned[:, HALF:], 1, y)
    plane = lax.all_gather(jnp.concatenate([row, column]), "fsdp", axis_index_groups=lines(0))

    scale, left, right = make_terms(at, tokens, cotangent)
    left_a, left_b = reduce_large(left, 1)
    right_a, right_b = reduce_large(right, 2)
    reduced = jnp.concatenate(
        [jnp.concatenate([left_a, right_a], axis=1), jnp.concatenate([left_b, right_b], axis=1)]
    )
    reduced = lax.psum_scatter(reduced, "fsdp", scatter_dimension=0, axis_index_groups=lines(0))

    pieces = gather_large(plane[:2, :SIDE], plane[2:, :SIDE], 1)
    pieces += gather_large(plane[:2, SIDE:], plane[2:, SIDE:], 2)
    values, token_grad = project(at, tokens, cotangent, scale, plane, pieces)

    summed = jnp.concatenate([reduce_small(reduced[:SIDE], 2, x), reduce_small(reduced[SIDE:], 1, y)]).T
    weight_grad = (summed * gain[:, None])[None]
    gain_grad = jnp.sum(summed * matrix, axis=1)[None]

    outer_new, momentum_new, local_new = outer_step(
        fragment_index, assignment, outer_params, momentum, local_params[0]
    )
    return (values, token_grad, weight_grad, gain_grad, outer_new, momentum_new, local_new[None])


def solution(mesh):
    in_specs = (
        P(("rep", "fsdp"), None),
        P(("rep", "fsdp"), None),
        P("rep", "fsdp", None),
        P("rep", "fsdp"),
        P(),
        P(),
        P(None, "fsdp"),
        P(None, "fsdp"),
        P("rep", None, "fsdp"),
    )
    out_specs = (
        P(("rep", "fsdp"), None),
        P(("rep", "fsdp"), None),
        P("rep", "fsdp", None),
        P("rep", "fsdp"),
        P(None, "fsdp"),
        P(None, "fsdp"),
        P("rep", None, "fsdp"),
    )
    return jax.shard_map(shards, mesh=mesh, in_specs=in_specs, out_specs=out_specs, check_vma=False)
```

```python
import jax
import jax.numpy as jnp
from jax import lax
from jax.experimental import pallas as pl
from jax.experimental.pallas import tpu as pltpu
from jax.sharding import PartitionSpec as P

NFRAG = 4
SIDE = 4
ROWS = 128
KV = 512
HALF = KV // 2
WIDE = SIDE * ROWS
VMEM_LIMIT = 56 * 1024 * 1024

epsilon = 1e-05
outer_rate = 0.7
nesterov = 0.9
mixing = 0.5


def flat(z, y, x):
    return (z * SIDE + y) * SIDE + x


def ring(axis, step):
    pairs = []
    for z in range(SIDE):
        for y in range(SIDE):
            for x in range(SIDE):
                to = [z, y, x]
                to[axis] = (to[axis] + step) % SIDE
                pairs.append((flat(z, y, x), flat(*to)))
    return pairs


def lines(axis):
    groups = []
    for a in range(SIDE):
        for b in range(SIDE):
            group = []
            for c in range(SIDE):
                at = [a, b]
                at.insert(axis, c)
                group.append(flat(*at))
            groups.append(group)
    return groups


def hop(value, axis, step):
    return lax.ppermute(value, "fsdp", ring(axis, step))


def stack_kernel(at, *refs):
    out = refs[-1]
    for d in range(SIDE):
        out[lax.rem(at[1] + d, SIDE)] = refs[d][...]
        out[SIDE + lax.rem(at[0] + d, SIDE)] = refs[SIDE + d][...]


def gather_small(at, row, column):
    parts = [row] + [hop(row, 2, -step) for step in (1, 2, 3)]
    parts += [column] + [hop(column, 1, -step) for step in (1, 2, 3)]
    vmem = pl.BlockSpec(memory_space=pltpu.VMEM)
    return pl.pallas_call(
        stack_kernel,
        out_shape=jax.ShapeDtypeStruct((2 * SIDE, ROWS, HALF), jnp.bfloat16),
        in_specs=[pl.BlockSpec(memory_space=pltpu.SMEM)] + [vmem] * (2 * SIDE),
        out_specs=vmem,
    )(at, *parts)


def gather_large(own, axis):
    before, after = hop(own, axis, 1), hop(own, axis, -1)
    far_a, far_b = hop(before[:2], axis, 1), hop(after[2:], axis, -1)
    return [after, far_a, far_b, before]


def total(*terms):
    return sum(t.astype(jnp.float32) for t in terms).astype(jnp.bfloat16)


def reduce_large(pieces, axis):
    own, after, before, far_a, far_b = pieces
    far_a, far_b = hop(far_a, axis, 1), hop(far_b, axis, -1)
    after = lax.dynamic_update_slice_in_dim(after, total(after[:2], far_a), 0, 0)
    before = lax.dynamic_update_slice_in_dim(before, total(before[2:], far_b), 2, 0)
    return [own, hop(after, axis, 1), hop(before, axis, -1)]


def tie(values, after):
    hbm = pl.BlockSpec(memory_space=pl.ANY)
    return pl.pallas_call(
        lambda *refs: None,
        out_shape=[jax.ShapeDtypeStruct(v.shape, v.dtype) for v in values],
        in_specs=[hbm] * (len(values) + 1),
        out_specs=[hbm] * len(values),
        input_output_aliases={i: i for i in range(len(values))},
    )(*values, after)


def reduce_small(term, axis, place):
    result = lax.dynamic_index_in_dim(term, place, 0, False).astype(jnp.float32)
    for step in (1, 2, 3):
        sent = lax.dynamic_index_in_dim(term, (place + step) % SIDE, 0, False)
        result = result + hop(sent, axis, step).astype(jnp.float32)
    return result


def place(outs, distance, z):
    return (outs[3 + z // 2], z % 2) if distance == 2 else (outs[(0, 1, None, 2)[distance]], z)


def terms_kernel(at, x_ref, cot_ref, scale_ref, *rest):
    outs, (turned, block) = (rest[:5], rest[5:10]), rest[10:]
    width = x_ref.shape[1]
    squares = jnp.zeros((x_ref.shape[0], ROWS), jnp.float32)
    for j in range(width // ROWS):
        part = x_ref[:, j * ROWS : (j + 1) * ROWS].astype(jnp.float32)
        squares = squares + part * part
    mean = jnp.sum(squares, axis=-1, keepdims=True) / width
    scale = lax.rsqrt(mean + epsilon)
    scale_ref[...] = scale
    scaled = cot_ref[...].astype(jnp.float32) * scale
    turned[...] = scaled.T.astype(jnp.bfloat16)
    for z in range(SIDE):
        for dy in range(SIDE):
            y = lax.rem(at[0] + dy, SIDE)
            start = pl.multiple_of((z * SIDE + y) * WIDE, WIDE)
            product = jnp.dot(
                turned[...], x_ref[:, pl.ds(start, WIDE)], preferred_element_type=jnp.float32
            )
            out, level = place(outs[0], dy, z)
            for x in range(SIDE):
                out[level, x] = product[:HALF, x * ROWS : (x + 1) * ROWS].astype(jnp.bfloat16)
            block[...] = product[HALF:].astype(jnp.bfloat16)
            for dx in range(SIDE):
                x = lax.rem(at[1] + dx, SIDE)
                out, level = place(outs[1], dx, z)
                out[level, y] = block[:, pl.ds(pl.multiple_of(x * ROWS, ROWS), ROWS)]


def make_terms(at, tokens, cotangent):
    rows, width = tokens.shape
    pieces = [jax.ShapeDtypeStruct((d, SIDE, HALF, ROWS), jnp.bfloat16) for d in (4, 4, 4, 2, 2) * 2]
    vmem = pl.BlockSpec(memory_space=pltpu.VMEM)
    scale, *pieces = pl.pallas_call(
        terms_kernel,
        out_shape=[jax.ShapeDtypeStruct((rows, 1), jnp.float32)] + pieces,
        in_specs=[pl.BlockSpec(memory_space=pltpu.SMEM), vmem, vmem],
        out_specs=[vmem] * 11,
        scratch_shapes=[pltpu.VMEM((KV, rows), jnp.bfloat16), pltpu.VMEM((HALF, WIDE), jnp.bfloat16)],
        compiler_params=pltpu.CompilerParams(vmem_limit_bytes=VMEM_LIMIT),
        cost_estimate=pl.CostEstimate(
            flops=2 * rows * width * KV, bytes_accessed=2 * width * (rows + KV), transcendentals=rows
        ),
    )(at, tokens, cotangent)
    return scale, pieces[:5], pieces[5:]


def sum_kernel(*refs):
    left, right, out = refs[:3], refs[3:6], refs[-1]
    for z in range(SIDE):
        for j in range(SIDE):
            for h, terms in enumerate((left, right)):
                value = terms[0][z, j].astype(jnp.float32)
                for term in terms[1:]:
                    value = value + term[z, j].astype(jnp.float32)
                out[z, h * SIDE + j] = value.astype(jnp.bfloat16)


def sum_terms(left, right, after):
    vmem = pl.BlockSpec(memory_space=pltpu.VMEM)
    return pl.pallas_call(
        sum_kernel,
        out_shape=jax.ShapeDtypeStruct((SIDE, 2 * SIDE, HALF, ROWS), jnp.bfloat16),
        in_specs=[vmem] * 6 + [pl.BlockSpec(memory_space=pl.ANY)],
        out_specs=vmem,
        compiler_params=pltpu.CompilerParams(vmem_limit_bytes=VMEM_LIMIT),
    )(*left, *right, after)


def project_kernel(at, x_ref, cot_ref, scale_ref, plane, *rest):
    pieces, (values_ref, grad_ref), (first, second) = (rest[:4], rest[4:8]), rest[8:10], rest[10:]
    width = x_ref.shape[1]
    for z in range(SIDE):
        for d in range(SIDE):
            y, x = lax.rem(at[0] + d, SIDE), lax.rem(at[1] + d, SIDE)
            for j in range(SIDE):
                if d == 0:
                    first[z, y, j] = plane[z, j]
                    second[z, j, x] = plane[z, SIDE + j]
                elif d == 2:
                    first[z, y, j] = pieces[0][1 + z // 2][z % 2, j]
                    second[z, j, x] = pieces[1][1 + z // 2][z % 2, j]
                else:
                    first[z, y, j] = pieces[0][d // 3 * 3][z, j]
                    second[z, j, x] = pieces[1][d // 3 * 3][z, j]
    scale = scale_ref[...]
    depth = SIDE * WIDE
    mean = jnp.zeros_like(scale)
    for h, matrix in enumerate((first, second)):
        columns = slice(h * HALF, (h + 1) * HALF)
        product = jnp.zeros((x_ref.shape[0], HALF), jnp.float32)
        for z in range(SIDE):
            product = product + jnp.dot(
                x_ref[:, z * depth : (z + 1) * depth],
                matrix[z].reshape(depth, HALF),
                preferred_element_type=jnp.float32,
            )
        values_ref[:, columns] = (product * scale).astype(jnp.bfloat16)
        mean = mean + jnp.sum(product * cot_ref[:, columns].astype(jnp.float32), axis=-1, keepdims=True)
    slope = scale * scale * scale * (mean / width)
    by_columns = (((1,), (1,)), ((), ()))
    for z in range(SIDE):
        for y in range(SIDE):
            weighted = lax.dot_general(
                cot_ref[:, :HALF], first[z, y].reshape(WIDE, HALF), by_columns, preferred_element_type=jnp.float32
            ) + lax.dot_general(
                cot_ref[:, HALF:], second[z, y].reshape(WIDE, HALF), by_columns, preferred_element_type=jnp.float32
            )
            start = (z * SIDE + y) * WIDE
            columns = slice(start, start + WIDE)
            grad_ref[:, columns] = (
                scale * weighted - x_ref[:, columns].astype(jnp.float32) * slope
            ).astype(jnp.bfloat16)


def project(at, tokens, cotangent, scale, plane, pieces):
    rows, width = tokens.shape
    vmem = pl.BlockSpec(memory_space=pltpu.VMEM)
    whole = pltpu.VMEM((SIDE, SIDE, SIDE, ROWS, HALF), jnp.bfloat16)
    return pl.pallas_call(
        project_kernel,
        out_shape=[
            jax.ShapeDtypeStruct((rows, KV), jnp.bfloat16),
            jax.ShapeDtypeStruct((rows, width), jnp.bfloat16),
        ],
        in_specs=[pl.BlockSpec(memory_space=pltpu.SMEM)] + [vmem] * 12,
        out_specs=[vmem] * 2,
        scratch_shapes=[whole, whole],
        compiler_params=pltpu.CompilerParams(vmem_limit_bytes=VMEM_LIMIT),
        cost_estimate=pl.CostEstimate(
            flops=4 * rows * width * KV, bytes_accessed=2 * width * (2 * rows + KV), transcendentals=0
        ),
    )(at, tokens, cotangent, scale, plane, *pieces)


def outer_step(fragment_index, assignment, outer_params, momentum, local, after):
    layers = assignment.shape[0]
    selected = assignment == jnp.remainder(fragment_index[0], NFRAG)
    one = jnp.argmax(selected)
    two = layers - 1 - jnp.argmax(selected[::-1])
    (chosen,) = tie([jnp.stack([lax.dynamic_index_in_dim(local, i, 0, False) for i in (one, two)])], after)
    replicas = lax.axis_size("rep")
    chip = jnp.stack([chosen, lax.ppermute(chosen, "rep", [(r, r ^ 1) for r in range(replicas)])])
    away = lax.ppermute(chip, "rep", [(r, r ^ 2) for r in range(replicas)])
    summed = jnp.sum(chip.astype(jnp.float32) + away.astype(jnp.float32), axis=0)
    spread = jnp.where((jnp.arange(layers) == one)[:, None], summed[0][None], summed[1][None])
    outer_delta = (replicas * outer_params - spread) / replicas
    momentum_new = jnp.where(selected[:, None], nesterov * momentum + outer_delta, momentum)
    outer_new = jnp.where(
        selected[:, None],
        outer_params - outer_rate * (outer_delta + nesterov * momentum_new),
        outer_params,
    )
    blended = (mixing * local.astype(jnp.float32) + (1.0 - mixing) * outer_new).astype(jnp.bfloat16)
    return outer_new, momentum_new, jnp.where(selected[:, None], blended, local)


def shards(
    tokens,
    cotangent,
    weight,
    norm_gain,
    fragment_index,
    assignment,
    outer_params,
    momentum,
    local_params,
):
    index = lax.axis_index("fsdp")
    y, x = (index // SIDE) % SIDE, index % SIDE
    at = jnp.stack([y, x]).astype(jnp.int32)
    gain = norm_gain[0].astype(jnp.float32)
    matrix = weight[0].astype(jnp.float32)
    row, column = ((matrix[:, h : h + HALF] * gain[:, None]).astype(jnp.bfloat16) for h in (0, HALF))

    cross = gather_small(at, row, column)
    plane = lax.all_gather(cross, "fsdp", axis_index_groups=lines(0))

    scale, left, right = make_terms(at, tokens, cotangent)
    left[3], left[4], right[3], right[4] = tie(left[3:] + right[3:], cross)
    left, right = reduce_large(left, 1), reduce_large(right, 2)
    reduced = sum_terms(left, right, plane)
    scattered = lax.psum_scatter(reduced, "fsdp", scatter_dimension=0, axis_index_groups=lines(0))

    pieces = gather_large(plane[:, :SIDE], 1) + gather_large(plane[:, SIDE:], 2)
    values, token_grad = project(at, tokens, cotangent, scale, plane, pieces)

    summed = jnp.concatenate([reduce_small(scattered[:SIDE], 2, x), reduce_small(scattered[SIDE:], 1, y)]).T
    weight_grad = (summed * gain[:, None])[None]
    gain_grad = jnp.sum(summed * matrix, axis=1)[None]

    outer_new, momentum_new, local_new = outer_step(
        fragment_index, assignment, outer_params, momentum, local_params[0], reduced
    )
    return (values, token_grad, weight_grad, gain_grad, outer_new, momentum_new, local_new[None])


def solution(mesh):
    in_specs = (
        P(("rep", "fsdp"), None),
        P(("rep", "fsdp"), None),
        P("rep", "fsdp", None),
        P("rep", "fsdp"),
        P(),
        P(),
        P(None, "fsdp"),
        P(None, "fsdp"),
        P("rep", None, "fsdp"),
    )
    out_specs = (
        P(("rep", "fsdp"), None),
        P(("rep", "fsdp"), None),
        P("rep", "fsdp", None),
        P("rep", "fsdp"),
        P(None, "fsdp"),
        P(None, "fsdp"),
        P("rep", None, "fsdp"),
    )
    return jax.shard_map(shards, mesh=mesh, in_specs=in_specs, out_specs=out_specs, check_vma=False)
```

```python
import jax
import jax.numpy as jnp
from jax import lax
from jax.experimental import pallas as pl
from jax.experimental.pallas import tpu as pltpu
from jax.sharding import PartitionSpec as P

NFRAG = 4
SIDE = 4
ROWS = 128
KV = 512
HALF = KV // 2
WIDE = SIDE * ROWS
VMEM = pl.BlockSpec(memory_space=pltpu.VMEM)
SMEM = pl.BlockSpec(memory_space=pltpu.SMEM)
ANY = pl.BlockSpec(memory_space=pl.ANY)

epsilon = 1e-05
outer_rate = 0.7
nesterov = 0.9
mixing = 0.5


def grant(mebibytes):
    return pltpu.CompilerParams(vmem_limit_bytes=mebibytes * 2**20)


def flat(z, y, x):
    return (z * SIDE + y) * SIDE + x


def ring(axis, step):
    pairs = []
    for z in range(SIDE):
        for y in range(SIDE):
            for x in range(SIDE):
                to = [z, y, x]
                to[axis] = (to[axis] + step) % SIDE
                pairs.append((flat(z, y, x), flat(*to)))
    return pairs


GRAY = (0, 1, 3, 2)


def z_ring():
    pairs = []
    for place, z in enumerate(GRAY):
        for y in range(SIDE):
            for x in range(SIDE):
                pairs.append((flat(z, y, x), flat(GRAY[(place + 1) % SIDE], y, x)))
    return pairs


def hop_z(value):
    return lax.ppermute(value, "fsdp", z_ring())


def hop(value, axis, step):
    return lax.ppermute(value, "fsdp", ring(axis, step))


def find(fragment_index, assignment):
    current = lax.rem(lax.rem(fragment_index[0], NFRAG) + NFRAG, NFRAG)
    one, two = jnp.int32(-1), jnp.int32(-1)
    for layer in range(assignment.shape[0]):
        chosen = assignment[layer] == current
        two = jnp.where(chosen & (one >= 0), layer, two)
        one = jnp.where(chosen & (one < 0), layer, one)
    return one, two


def choose_kernel(fragment_index, assignment, local, behind, chosen):
    del behind
    value = local[...].astype(jnp.float32)
    layer = lax.broadcasted_iota(jnp.int32, value.shape, 0)
    picks = [
        jnp.sum(jnp.where(layer == which, value, 0.0), axis=0, keepdims=True)
        for which in find(fragment_index, assignment)
    ]
    chosen[...] = jnp.concatenate(picks).astype(jnp.bfloat16)


def choose(fragment_index, assignment, local, behind):
    return pl.pallas_call(
        choose_kernel,
        out_shape=jax.ShapeDtypeStruct((2, local.shape[1]), jnp.bfloat16),
        in_specs=[SMEM, SMEM, VMEM, ANY],
        out_specs=VMEM,
        compiler_params=grant(4),
    )(fragment_index, assignment, local, behind)


def fold_kernel(weight_hbm, gain_hbm, row, column, weight, gain, sems):
    copies = [
        pltpu.make_async_copy(gain_hbm, gain, sems.at[0]),
        pltpu.make_async_copy(weight_hbm, weight, sems.at[1]),
    ]
    for copy in copies:
        copy.start()
    copies[0].wait()
    factor = jnp.broadcast_to(gain[...].astype(jnp.float32), (ROWS, ROWS)).T
    copies[1].wait()
    for j in range(KV // ROWS):
        part = (weight[:, j * ROWS : (j + 1) * ROWS].astype(jnp.float32) * factor).astype(jnp.bfloat16)
        out, at = (row, j * ROWS) if j * ROWS < HALF else (column, j * ROWS - HALF)
        out[:, at : at + ROWS] = part


def fold(weight, gain):
    half = jax.ShapeDtypeStruct((ROWS, HALF), jnp.bfloat16)
    return pl.pallas_call(
        fold_kernel,
        out_shape=[half, half],
        in_specs=[ANY] * 2,
        out_specs=[VMEM] * 2,
        scratch_shapes=[
            pltpu.VMEM(weight.shape, weight.dtype),
            pltpu.VMEM(gain.shape, gain.dtype),
            pltpu.SemaphoreType.DMA((2,)),
        ],
        compiler_params=grant(60),
    )(weight, gain)


def stack_kernel(at, *refs):
    out = refs[-1]
    for d in range(SIDE):
        out[lax.rem(at[1] + d, SIDE)] = refs[d][...]
        out[SIDE + lax.rem(at[0] + d, SIDE)] = refs[SIDE + d][...]


def gather_small(at, row, column, behind):
    parts = [row] + [hop(row, 2, -step) for step in (1, 2, 3)]
    parts += [column] + [hop(column, 1, -step) for step in (1, 2, 3)]
    return pl.pallas_call(
        stack_kernel,
        out_shape=jax.ShapeDtypeStruct((2 * SIDE, ROWS, HALF), jnp.bfloat16),
        in_specs=[SMEM] + [VMEM] * 8 + [ANY] * len(behind),
        out_specs=VMEM,
        compiler_params=grant(4),
    )(at, *parts, *behind)


def split_kernel(*refs):
    left, right = refs[SIDE:]
    for k, part in enumerate(refs[:SIDE]):
        left[k] = part[:SIDE]
        right[k] = part[SIDE:]


def split(parts):
    half = jax.ShapeDtypeStruct((SIDE, SIDE, ROWS, HALF), jnp.bfloat16)
    return pl.pallas_call(
        split_kernel,
        out_shape=[half, half],
        in_specs=[VMEM] * SIDE,
        out_specs=[VMEM] * 2,
        compiler_params=grant(8),
        cost_estimate=pl.CostEstimate(flops=0, bytes_accessed=4 * 2**20, transcendentals=0),
    )(*parts)


def halves_kernel(before, after, far_a, far_b):
    far_a[...] = before[...]
    far_b[...] = after[...]


def gather_large(own, axis):
    before, after = hop(own, axis, 1), hop(own, axis, -1)
    shape = (SIDE // 2, *own.shape[1:])
    half = jax.ShapeDtypeStruct(shape, own.dtype)
    far_a, far_b = pl.pallas_call(
        halves_kernel,
        grid=(1,),
        out_shape=[half, half],
        in_specs=[pl.BlockSpec(shape, lambda i: (0, 0, 0, 0)), pl.BlockSpec(shape, lambda i: (1, 0, 0, 0))],
        out_specs=[pl.BlockSpec(shape, lambda i: (0, 0, 0, 0))] * 2,
        compiler_params=grant(6),
        cost_estimate=pl.CostEstimate(flops=0, bytes_accessed=2 * 2**20, transcendentals=0),
    )(before, after)
    return [own, after, hop(far_a, axis, 1), hop(far_b, axis, -1), before], far_a


def pass_kernel(after, far_a, before, far_b, *rest):
    after_out, before_out = rest[-2:]
    after_out[...] = (after[...].astype(jnp.float32) + far_a[...].astype(jnp.float32)).astype(jnp.bfloat16)
    before_out[...] = (before[...].astype(jnp.float32) + far_b[...].astype(jnp.float32)).astype(jnp.bfloat16)


def pass_on(after, before, far_a, far_b, behind):
    whole = jax.ShapeDtypeStruct(after.shape, after.dtype)
    low = pl.BlockSpec((1, SIDE, HALF, ROWS), lambda z: (z, 0, 0, 0))
    high = pl.BlockSpec((1, SIDE, HALF, ROWS), lambda z: (2 + z, 0, 0, 0))
    return pl.pallas_call(
        pass_kernel,
        grid=(2,),
        out_shape=[whole, whole],
        in_specs=[low, low, high, low, ANY],
        out_specs=[low, high],
        input_output_aliases={0: 0, 2: 1},
        compiler_params=grant(6),
        cost_estimate=pl.CostEstimate(flops=0, bytes_accessed=3 * 2**20, transcendentals=0),
    )(after, far_a, before, far_b, behind)


def reduce_large(far, near, axis, behind):
    own, after, before = near
    after, before = pass_on(after, before, hop(far[0], axis, 1), hop(far[1], axis, -1), behind)
    return [own, hop(after, axis, 1), hop(before, axis, -1)]


def reduce_small(term, axis, place):
    sent = [lax.dynamic_index_in_dim(term, (place + step) % SIDE, 0, False) for step in (1, 2, 3)]
    return [hop(value, axis, step) for step, value in zip((1, 2, 3), sent)]


def finish_kernel(at, weight, gain, scattered, *refs):
    arrived, (weight_grad, gain_grad) = refs[:6], refs[6:]
    row = gain[...].astype(jnp.float32)
    factor = jnp.broadcast_to(row, (ROWS, ROWS)).T
    total = jnp.zeros((1, ROWS), jnp.float32)
    for j in range(KV // ROWS):
        h, low = divmod(j * ROWS, HALF)
        where = at[1] if h == 0 else SIDE + at[0]
        part = scattered[where, low : low + ROWS].astype(jnp.float32)
        for term in arrived[3 * h : 3 * h + 3]:
            part = part + term[low : low + ROWS].astype(jnp.float32)
        columns = slice(j * ROWS, (j + 1) * ROWS)
        weight_grad[:, columns] = part.T * factor
        total = total + jnp.sum(part * weight[:, columns].astype(jnp.float32).T, axis=0, keepdims=True)
    gain_grad[...] = total


def finish(at, weight, gain, scattered, arrived):
    return pl.pallas_call(
        finish_kernel,
        out_shape=[jax.ShapeDtypeStruct((ROWS, KV), jnp.float32), jax.ShapeDtypeStruct((1, ROWS), jnp.float32)],
        in_specs=[SMEM] + [VMEM] * 9,
        out_specs=[VMEM] * 2,
        compiler_params=grant(6),
    )(at, weight, gain, scattered, *arrived)


def columns_of(at, x_ref, distance, picked):
    x = lax.rem(at[1] + distance, SIDE)
    for y in range(SIDE):
        picked[:, y * ROWS : (y + 1) * ROWS] = x_ref[:, pl.ds(pl.multiple_of(y * WIDE + x * ROWS, ROWS), ROWS)]
    return picked[...]


def terms_of(at, turned, x_ref, distance, picked, left, right):
    start = pl.multiple_of(lax.rem(at[0] + distance, SIDE) * WIDE, WIDE)
    for h, columns, out in (
        (0, x_ref[:, pl.ds(start, WIDE)], left),
        (1, columns_of(at, x_ref, distance, picked), right),
    ):
        product = jnp.dot(
            turned[h * HALF : (h + 1) * HALF], columns, preferred_element_type=jnp.float32
        ).astype(jnp.bfloat16)
        for j in range(SIDE):
            out[0, j] = product[:, j * ROWS : (j + 1) * ROWS]


def far_kernel(at, x_hbm, cot_hbm, scale_ref, turned, left_a, left_b, right_a, right_b, x_ref, cot_ref, picked, sems):
    rows, width = x_ref.shape
    depth = width // SIDE
    quarters = [slice(z * depth, (z + 1) * depth) for z in range(SIDE)]
    copies = [pltpu.make_async_copy(x_hbm.at[:, q], x_ref.at[:, q], sems.at[z]) for z, q in enumerate(quarters)]
    copies.append(pltpu.make_async_copy(cot_hbm, cot_ref, sems.at[SIDE]))
    for copy in copies:
        copy.start()
    squares = jnp.zeros((rows, ROWS), jnp.float32)
    for z in range(SIDE):
        copies[z].wait()
        for j in range(depth // ROWS):
            start = z * depth + j * ROWS
            part = x_ref[:, start : start + ROWS].astype(jnp.float32)
            squares = squares + part * part
    mean = jnp.sum(squares, axis=-1, keepdims=True) / width
    scale = lax.rsqrt(mean + epsilon)
    scale_ref[...] = scale
    copies[SIDE].wait()
    turned[...] = (cot_ref[...].astype(jnp.float32) * scale).T.astype(jnp.bfloat16)
    for z in range(SIDE):
        left, right = ((left_a, right_a), (left_b, right_b))[z // 2]
        level = pl.ds(z % 2, 1)
        terms_of(at, turned, x_ref.at[:, quarters[z]], 2, picked, left.at[level], right.at[level])


def make_far(at, tokens, cotangent):
    rows, width = tokens.shape
    scale, turned, *far = pl.pallas_call(
        far_kernel,
        out_shape=[jax.ShapeDtypeStruct((rows, 1), jnp.float32), jax.ShapeDtypeStruct((KV, rows), jnp.bfloat16)]
        + [jax.ShapeDtypeStruct((2, SIDE, HALF, ROWS), jnp.bfloat16)] * 4,
        in_specs=[SMEM, ANY, ANY],
        out_specs=[VMEM] * 6,
        scratch_shapes=[
            pltpu.VMEM((rows, width), jnp.bfloat16),
            pltpu.VMEM((rows, KV), jnp.bfloat16),
            pltpu.VMEM((rows, WIDE), jnp.bfloat16),
            pltpu.SemaphoreType.DMA((SIDE + 1,)),
        ],
        compiler_params=grant(59),
        cost_estimate=pl.CostEstimate(
            flops=rows * width * KV // 2, bytes_accessed=2 * width * (rows + KV // 4), transcendentals=rows
        ),
    )(at, tokens, cotangent)
    return scale, turned, far[:2], far[2:]


def near_kernel(at, turned, x_ref, behind, *refs):
    del behind
    picked = refs[-1]
    for i, distance in enumerate((0, 1, 3)):
        terms_of(at, turned, x_ref, distance, picked, refs[i], refs[3 + i])


def make_near(at, turned, tokens, behind):
    rows, width = tokens.shape
    near = pl.pallas_call(
        near_kernel,
        grid=(SIDE,),
        out_shape=[jax.ShapeDtypeStruct((SIDE, SIDE, HALF, ROWS), jnp.bfloat16)] * 6,
        in_specs=[
            SMEM,
            pl.BlockSpec((KV, rows), lambda z: (0, 0)),
            pl.BlockSpec((rows, width // SIDE), lambda z: (0, z)),
            ANY,
        ],
        out_specs=[pl.BlockSpec((1, SIDE, HALF, ROWS), lambda z: (z, 0, 0, 0))] * 6,
        scratch_shapes=[pltpu.VMEM((rows, WIDE), jnp.bfloat16)],
        compiler_params=grant(54),
        cost_estimate=pl.CostEstimate(
            flops=3 * rows * width * KV // 2,
            bytes_accessed=2 * width * (rows + 3 * KV // 4),
            transcendentals=0,
        ),
    )(at, turned, tokens, behind)
    return near[:3], near[3:]


def sum_kernel(at, *refs):
    del at
    out = refs[7]
    for h, terms in enumerate((refs[:3], refs[3:6])):
        for j in range(SIDE):
            value = terms[0][0, j].astype(jnp.float32)
            for term in terms[1:]:
                value = value + term[0, j].astype(jnp.float32)
            out[0, h * SIDE + j] = value.astype(jnp.bfloat16)


def sum_terms(at, terms, behind, first, count):
    level = pl.BlockSpec(
        (1, SIDE, HALF, ROWS), lambda i, at: (at[2 + lax.rem(first + i, SIDE)], 0, 0, 0)
    )
    return pl.pallas_call(
        sum_kernel,
        grid_spec=pltpu.PrefetchScalarGridSpec(
            num_scalar_prefetch=1,
            grid=(count,),
            in_specs=[level] * 6 + [ANY],
            out_specs=pl.BlockSpec((1, 2 * SIDE, HALF, ROWS), lambda i, at: (i, 0, 0, 0)),
        ),
        out_shape=jax.ShapeDtypeStruct((count, 2 * SIDE, HALF, ROWS), jnp.bfloat16),
        compiler_params=grant(12),
        cost_estimate=pl.CostEstimate(flops=0, bytes_accessed=count * 2 * 2**20, transcendentals=0),
    )(at, *terms, behind)


def add_kernel(*refs):
    received, own, out = refs[0], refs[1], refs[-1]
    out[...] = (received[...].astype(jnp.float32) + own[0].astype(jnp.float32)).astype(jnp.bfloat16)


def add_own(received, rest, i, behind=()):
    whole = pl.BlockSpec(received.shape, lambda _: (0, 0, 0))
    return pl.pallas_call(
        add_kernel,
        grid=(1,),
        out_shape=jax.ShapeDtypeStruct(received.shape, received.dtype),
        in_specs=[whole, pl.BlockSpec((1, *received.shape), lambda _: (i, 0, 0, 0))] + [ANY] * len(behind),
        out_specs=whole,
        compiler_params=grant(6),
        cost_estimate=pl.CostEstimate(flops=0, bytes_accessed=2 * 2**20, transcendentals=0),
    )(received, rest, *behind)


def reduce_z(at, terms, behind, last_behind):
    moving = sum_terms(at, terms, behind, 1, 1)[0]
    rest = sum_terms(at, terms, behind, 2, 3)
    moving = add_own(hop_z(moving), rest, 0)
    moving = add_own(hop_z(moving), rest, 1, last_behind)
    return add_own(hop_z(moving), rest, 2)


def project_kernel(at, x_hbm, cot_ref, scale_ref, *rest):
    pieces, (values_ref, grad_hbm), (x_ref, first, second, grad, sems, out_sems) = (rest[:5], rest[5:10]), rest[10:12], rest[12:]
    rows, width = x_ref.shape
    depth = width // SIDE
    copies, blocks = [], []
    for k in range(SIDE):
        z = at[2 + k]
        columns = pl.ds(pl.multiple_of(z * depth, depth), depth)
        blocks.append((z, columns))
        moves = [(x_hbm.at[:, columns], x_ref.at[:, columns])]
        for d in range(SIDE):
            y, x = lax.rem(at[0] + d, SIDE), lax.rem(at[1] + d, SIDE)
            for h in range(2):
                own, after, far_a, far_b, before = pieces[h]
                if d == 2:
                    source = (far_a, far_b)[k // 2].at[k % 2]
                else:
                    source = (own, after, None, before)[d].at[k]
                moves.append((source, first.at[z, y] if h == 0 else second.at[z, :, x]))
        copies.append([pltpu.make_async_copy(a, b, sems.at[k, i]) for i, (a, b) in enumerate(moves)])
        for copy in copies[-1]:
            copy.start()
    scale = scale_ref[...]
    products = [jnp.zeros((rows, HALF), jnp.float32)] * 2
    for k, (z, columns) in enumerate(blocks):
        for copy in copies[k]:
            copy.wait()
        block = x_ref[:, columns]
        products = [
            product + jnp.dot(block, matrix[z].reshape(depth, HALF), preferred_element_type=jnp.float32)
            for product, matrix in zip(products, (first, second))
        ]
    mean = jnp.zeros_like(scale)
    for h, product in enumerate(products):
        columns = slice(h * HALF, (h + 1) * HALF)
        values_ref[:, columns] = (product * scale).astype(jnp.bfloat16)
        mean = mean + jnp.sum(product * cot_ref[:, columns].astype(jnp.float32), axis=-1, keepdims=True)
    slope = scale * scale * scale * (mean / width)
    by_columns = (((1,), (1,)), ((), ()))
    copies = []
    for z in range(SIDE):
        for y in range(SIDE):
            weighted = lax.dot_general(
                cot_ref[:, :HALF], first[z, y].reshape(WIDE, HALF), by_columns, preferred_element_type=jnp.float32
            ) + lax.dot_general(
                cot_ref[:, HALF:], second[z, y].reshape(WIDE, HALF), by_columns, preferred_element_type=jnp.float32
            )
            start = (z * SIDE + y) * WIDE
            columns = slice(start, start + WIDE)
            grad[:, columns] = (scale * weighted - x_ref[:, columns].astype(jnp.float32) * slope).astype(jnp.bfloat16)
        columns = slice(z * depth, (z + 1) * depth)
        copies.append(pltpu.make_async_copy(grad.at[:, columns], grad_hbm.at[:, columns], out_sems.at[z]))
        copies[-1].start()
    for copy in copies:
        copy.wait()


def project(at, tokens, cotangent, scale, pieces):
    rows, width = tokens.shape
    whole = pltpu.VMEM((SIDE, SIDE, SIDE, ROWS, HALF), jnp.bfloat16)
    return pl.pallas_call(
        project_kernel,
        out_shape=[
            jax.ShapeDtypeStruct((rows, KV), jnp.bfloat16),
            jax.ShapeDtypeStruct((rows, width), jnp.bfloat16),
        ],
        in_specs=[SMEM, ANY, VMEM, VMEM] + [ANY] * 10,
        out_specs=[VMEM, ANY],
        scratch_shapes=[
            pltpu.VMEM((rows, width), jnp.bfloat16),
            whole,
            whole,
            pltpu.VMEM((rows, width), jnp.bfloat16),
            pltpu.SemaphoreType.DMA((SIDE, 9)),
            pltpu.SemaphoreType.DMA((SIDE,)),
        ],
        compiler_params=grant(53),
        cost_estimate=pl.CostEstimate(
            flops=64 * rows * width * KV, bytes_accessed=2 * width * (2 * rows + KV), transcendentals=0
        ),
    )(at, tokens, cotangent, scale, *pieces)


def outer_kernel(fragment_index, assignment, outer, momentum, local, chip, away, outer_out, momentum_out, local_out):
    one, two = find(fragment_index, assignment)
    params, old, mine = outer[...], momentum[...], local[...].astype(jnp.float32)
    summed = chip[...].astype(jnp.float32) + away[...].astype(jnp.float32)
    summed = summed[:2] + summed[2:]
    layer = lax.broadcasted_iota(jnp.int32, params.shape, 0)
    spread = jnp.where(layer == one, summed[0:1], summed[1:2])
    selected = (layer == one) | (layer == two)
    delta = (4.0 * params - spread) / 4.0
    new = nesterov * old + delta
    step = params - outer_rate * (delta + nesterov * new)
    momentum_out[...] = jnp.where(selected, new, old)
    outer_out[...] = jnp.where(selected, step, params)
    local_out[...] = jnp.where(selected, mixing * mine + (1.0 - mixing) * step, mine).astype(jnp.bfloat16)


def outer_step(fragment_index, assignment, outer_params, momentum, local, behind):
    chosen = choose(fragment_index, assignment, local, behind)
    replicas = lax.axis_size("rep")
    chip = jnp.concatenate([chosen, lax.ppermute(chosen, "rep", [(r, r ^ 1) for r in range(replicas)])])
    away = lax.ppermute(chip, "rep", [(r, r ^ 2) for r in range(replicas)])
    return pl.pallas_call(
        outer_kernel,
        out_shape=[
            jax.ShapeDtypeStruct(outer_params.shape, jnp.float32),
            jax.ShapeDtypeStruct(momentum.shape, jnp.float32),
            jax.ShapeDtypeStruct(local.shape, jnp.bfloat16),
        ],
        in_specs=[SMEM, SMEM] + [VMEM] * 5,
        out_specs=[VMEM] * 3,
        compiler_params=grant(8),
    )(fragment_index, assignment, outer_params, momentum, local, chip, away)


def shards(
    tokens,
    cotangent,
    weight,
    norm_gain,
    fragment_index,
    assignment,
    outer_params,
    momentum,
    local_params,
):
    index = lax.axis_index("fsdp")
    z, y, x = index // (SIDE * SIDE), (index // SIDE) % SIDE, index % SIDE
    ring_place = z ^ (z >> 1)
    quarters = [(ring_place - k) & (SIDE - 1) for k in range(SIDE)]
    at = jnp.stack([y, x] + [q ^ (q >> 1) for q in quarters]).astype(jnp.int32)

    row, column = fold(weight[0], norm_gain)
    scale, turned, left_far, right_far = make_far(at, tokens, cotangent)
    cross = gather_small(at, row, column, [turned])
    quarter = [cross]
    for _ in range(SIDE - 1):
        quarter.append(hop_z(quarter[-1]))
    plane, other = split(quarter)

    left, right = make_near(at, turned, tokens, cross)
    terms = reduce_large(left_far, left, 1, quarter[1]) + reduce_large(right_far, right, 2, quarter[1])

    pieces, sent = zip(gather_large(plane, 1), gather_large(other, 2))
    scattered = reduce_z(at, terms, plane, sent)
    values, token_grad = project(at, tokens, cotangent, scale, pieces[0] + pieces[1])

    arrived = reduce_small(scattered[:SIDE], 2, x) + reduce_small(scattered[SIDE:], 1, y)
    weight_grad, gain_grad = finish(at, weight[0], norm_gain, scattered, arrived)

    outer_new, momentum_new, local_new = outer_step(
        fragment_index, assignment, outer_params, momentum, local_params[0], pieces[1][2]
    )
    return (values, token_grad, weight_grad[None], gain_grad, outer_new, momentum_new, local_new[None])


def solution(mesh):
    in_specs = (
        P(("rep", "fsdp"), None),
        P(("rep", "fsdp"), None),
        P("rep", "fsdp", None),
        P("rep", "fsdp"),
        P(),
        P(),
        P(None, "fsdp"),
        P(None, "fsdp"),
        P("rep", None, "fsdp"),
    )
    out_specs = (
        P(("rep", "fsdp"), None),
        P(("rep", "fsdp"), None),
        P("rep", "fsdp", None),
        P("rep", "fsdp"),
        P(None, "fsdp"),
        P(None, "fsdp"),
        P("rep", None, "fsdp"),
    )
    return jax.shard_map(shards, mesh=mesh, in_specs=in_specs, out_specs=out_specs, check_vma=False)
```

```python
import jax
import jax.numpy as jnp
from jax import lax
from jax.experimental import pallas as pl
from jax.experimental.pallas import tpu as pltpu
from jax.sharding import PartitionSpec as P

NFRAG = 4
SIDE = 4
ROWS = 128
KV = 512
HALF = KV // 2
WIDE = SIDE * ROWS
VMEM = pl.BlockSpec(memory_space=pltpu.VMEM)
SMEM = pl.BlockSpec(memory_space=pltpu.SMEM)
ANY = pl.BlockSpec(memory_space=pl.ANY)

epsilon = 1e-05
outer_rate = 0.7
nesterov = 0.9
mixing = 0.5


def grant(mebibytes):
    return pltpu.CompilerParams(vmem_limit_bytes=mebibytes * 2**20)


def flat(z, y, x):
    return (z * SIDE + y) * SIDE + x


def ring(axis, step):
    pairs = []
    for z in range(SIDE):
        for y in range(SIDE):
            for x in range(SIDE):
                to = [z, y, x]
                to[axis] = (to[axis] + step) % SIDE
                pairs.append((flat(z, y, x), flat(*to)))
    return pairs


GRAY = (0, 1, 3, 2)


def z_ring():
    pairs = []
    for place, z in enumerate(GRAY):
        for y in range(SIDE):
            for x in range(SIDE):
                pairs.append((flat(z, y, x), flat(GRAY[(place + 1) % SIDE], y, x)))
    return pairs


def hop_z(value):
    return lax.ppermute(value, "fsdp", z_ring())


def hop(value, axis, step):
    return lax.ppermute(value, "fsdp", ring(axis, step))


def find(fragment_index, assignment):
    current = lax.rem(lax.rem(fragment_index[0], NFRAG) + NFRAG, NFRAG)
    one, two = jnp.int32(-1), jnp.int32(-1)
    for layer in range(assignment.shape[0]):
        chosen = assignment[layer] == current
        two = jnp.where(chosen & (one >= 0), layer, two)
        one = jnp.where(chosen & (one < 0), layer, one)
    return one, two


def choose_kernel(fragment_index, assignment, local, behind, chosen):
    del behind
    value = local[...].astype(jnp.float32)
    layer = lax.broadcasted_iota(jnp.int32, value.shape, 0)
    picks = [
        jnp.sum(jnp.where(layer == which, value, 0.0), axis=0, keepdims=True)
        for which in find(fragment_index, assignment)
    ]
    chosen[...] = jnp.concatenate(picks).astype(jnp.bfloat16)


def choose(fragment_index, assignment, local, behind):
    return pl.pallas_call(
        choose_kernel,
        out_shape=jax.ShapeDtypeStruct((2, local.shape[1]), jnp.bfloat16),
        in_specs=[SMEM, SMEM, VMEM, ANY],
        out_specs=VMEM,
        compiler_params=grant(4),
    )(fragment_index, assignment, local, behind)


def fold_kernel(weight_hbm, gain_hbm, row, column, weight, gain, sems):
    copies = [
        pltpu.make_async_copy(gain_hbm, gain, sems.at[0]),
        pltpu.make_async_copy(weight_hbm, weight, sems.at[1]),
    ]
    for copy in copies:
        copy.start()
    copies[0].wait()
    factor = jnp.broadcast_to(gain[...].astype(jnp.float32), (ROWS, ROWS)).T
    copies[1].wait()
    for j in range(KV // ROWS):
        part = (weight[:, j * ROWS : (j + 1) * ROWS].astype(jnp.float32) * factor).astype(jnp.bfloat16)
        out, at = (row, j * ROWS) if j * ROWS < HALF else (column, j * ROWS - HALF)
        out[:, at : at + ROWS] = part


def fold(weight, gain):
    half = jax.ShapeDtypeStruct((ROWS, HALF), jnp.bfloat16)
    return pl.pallas_call(
        fold_kernel,
        out_shape=[half, half],
        in_specs=[ANY] * 2,
        out_specs=[VMEM] * 2,
        scratch_shapes=[
            pltpu.VMEM(weight.shape, weight.dtype),
            pltpu.VMEM(gain.shape, gain.dtype),
            pltpu.SemaphoreType.DMA((2,)),
        ],
        compiler_params=grant(60),
    )(weight, gain)


def stack_kernel(at, *refs):
    out = refs[-1]
    for d in range(SIDE):
        out[lax.rem(at[1] + d, SIDE)] = refs[d][...]
        out[SIDE + lax.rem(at[0] + d, SIDE)] = refs[SIDE + d][...]


def gather_small(at, row, column, behind):
    parts = [row] + [hop(row, 2, -step) for step in (1, 2, 3)]
    parts += [column] + [hop(column, 1, -step) for step in (1, 2, 3)]
    return pl.pallas_call(
        stack_kernel,
        out_shape=jax.ShapeDtypeStruct((2 * SIDE, ROWS, HALF), jnp.bfloat16),
        in_specs=[SMEM] + [VMEM] * 8 + [ANY] * len(behind),
        out_specs=VMEM,
        compiler_params=grant(4),
    )(at, *parts, *behind)


def split_kernel(*refs):
    left, right = refs[SIDE:]
    for k, part in enumerate(refs[:SIDE]):
        left[k] = part[:SIDE]
        right[k] = part[SIDE:]


def split(parts):
    half = jax.ShapeDtypeStruct((SIDE, SIDE, ROWS, HALF), jnp.bfloat16)
    return pl.pallas_call(
        split_kernel,
        out_shape=[half, half],
        in_specs=[VMEM] * SIDE,
        out_specs=[VMEM] * 2,
        compiler_params=grant(8),
        cost_estimate=pl.CostEstimate(flops=0, bytes_accessed=4 * 2**20, transcendentals=0),
    )(*parts)


def halves_kernel(before, after, far_a, far_b):
    far_a[...] = before[...]
    far_b[...] = after[...]


def gather_large(own, axis):
    before, after = hop(own, axis, 1), hop(own, axis, -1)
    shape = (SIDE // 2, *own.shape[1:])
    half = jax.ShapeDtypeStruct(shape, own.dtype)
    far_a, far_b = pl.pallas_call(
        halves_kernel,
        grid=(1,),
        out_shape=[half, half],
        in_specs=[pl.BlockSpec(shape, lambda i: (0, 0, 0, 0)), pl.BlockSpec(shape, lambda i: (1, 0, 0, 0))],
        out_specs=[pl.BlockSpec(shape, lambda i: (0, 0, 0, 0))] * 2,
        compiler_params=grant(6),
        cost_estimate=pl.CostEstimate(flops=0, bytes_accessed=2 * 2**20, transcendentals=0),
    )(before, after)
    return [own, after, hop(far_a, axis, 1), hop(far_b, axis, -1), before], far_a


def pass_kernel(after, far_a, before, far_b, *rest):
    after_out, before_out = rest[-2:]
    after_out[...] = (after[...].astype(jnp.float32) + far_a[...].astype(jnp.float32)).astype(jnp.bfloat16)
    before_out[...] = (before[...].astype(jnp.float32) + far_b[...].astype(jnp.float32)).astype(jnp.bfloat16)


def pass_on(after, before, far_a, far_b, behind):
    whole = jax.ShapeDtypeStruct(after.shape, after.dtype)
    low = pl.BlockSpec((1, SIDE, HALF, ROWS), lambda z: (z, 0, 0, 0))
    high = pl.BlockSpec((1, SIDE, HALF, ROWS), lambda z: (2 + z, 0, 0, 0))
    return pl.pallas_call(
        pass_kernel,
        grid=(2,),
        out_shape=[whole, whole],
        in_specs=[low, low, high, low, ANY],
        out_specs=[low, high],
        input_output_aliases={0: 0, 2: 1},
        compiler_params=grant(6),
        cost_estimate=pl.CostEstimate(flops=0, bytes_accessed=3 * 2**20, transcendentals=0),
    )(after, far_a, before, far_b, behind)


def reduce_large(far, near, axis, behind):
    own, after, before = near
    after, before = pass_on(after, before, hop(far[0], axis, 1), hop(far[1], axis, -1), behind)
    return [own, hop(after, axis, 1), hop(before, axis, -1)]


def reduce_small(term, axis, place):
    sent = [lax.dynamic_index_in_dim(term, (place + step) % SIDE, 0, False) for step in (1, 2, 3)]
    return [hop(value, axis, step) for step, value in zip((1, 2, 3), sent)]


def finish_kernel(at, weight, gain, scattered, *refs):
    arrived, (weight_grad, gain_grad) = refs[:6], refs[6:]
    row = gain[...].astype(jnp.float32)
    factor = jnp.broadcast_to(row, (ROWS, ROWS)).T
    total = jnp.zeros((1, ROWS), jnp.float32)
    for j in range(KV // ROWS):
        h, low = divmod(j * ROWS, HALF)
        where = at[1] if h == 0 else SIDE + at[0]
        part = scattered[where, low : low + ROWS].astype(jnp.float32)
        for term in arrived[3 * h : 3 * h + 3]:
            part = part + term[low : low + ROWS].astype(jnp.float32)
        columns = slice(j * ROWS, (j + 1) * ROWS)
        weight_grad[:, columns] = part.T * factor
        total = total + jnp.sum(part * weight[:, columns].astype(jnp.float32).T, axis=0, keepdims=True)
    gain_grad[...] = total


def finish(at, weight, gain, scattered, arrived):
    return pl.pallas_call(
        finish_kernel,
        out_shape=[jax.ShapeDtypeStruct((ROWS, KV), jnp.float32), jax.ShapeDtypeStruct((1, ROWS), jnp.float32)],
        in_specs=[SMEM] + [VMEM] * 9,
        out_specs=[VMEM] * 2,
        compiler_params=grant(6),
    )(at, weight, gain, scattered, *arrived)


def columns_of(at, x_ref, distance, picked):
    x = lax.rem(at[1] + distance, SIDE)
    for y in range(SIDE):
        picked[:, y * ROWS : (y + 1) * ROWS] = x_ref[:, pl.ds(pl.multiple_of(y * WIDE + x * ROWS, ROWS), ROWS)]
    return picked[...]


def terms_of(at, turned, x_ref, distance, picked, left, right):
    start = pl.multiple_of(lax.rem(at[0] + distance, SIDE) * WIDE, WIDE)
    for h, columns, out in (
        (0, x_ref[:, pl.ds(start, WIDE)], left),
        (1, columns_of(at, x_ref, distance, picked), right),
    ):
        product = jnp.dot(
            turned[h * HALF : (h + 1) * HALF], columns, preferred_element_type=jnp.float32
        ).astype(jnp.bfloat16)
        for j in range(SIDE):
            out[0, j] = product[:, j * ROWS : (j + 1) * ROWS]


def far_kernel(at, x_ref, cot_ref, scale_ref, turned, left_a, left_b, right_a, right_b, picked):
    rows, width = x_ref.shape
    depth = width // SIDE
    quarters = [slice(z * depth, (z + 1) * depth) for z in range(SIDE)]
    squares = jnp.zeros((rows, ROWS), jnp.float32)
    for j in range(width // ROWS):
        part = x_ref[:, j * ROWS : (j + 1) * ROWS].astype(jnp.float32)
        squares = squares + part * part
    mean = jnp.sum(squares, axis=-1, keepdims=True) / width
    scale = lax.rsqrt(mean + epsilon)
    scale_ref[...] = scale
    turned[...] = (cot_ref[...].astype(jnp.float32) * scale).T.astype(jnp.bfloat16)
    for z in range(SIDE):
        left, right = ((left_a, right_a), (left_b, right_b))[z // 2]
        level = pl.ds(z % 2, 1)
        terms_of(at, turned, x_ref.at[:, quarters[z]], 2, picked, left.at[level], right.at[level])


def make_far(at, tokens, cotangent):
    rows, width = tokens.shape
    scale, turned, *far = pl.pallas_call(
        far_kernel,
        out_shape=[jax.ShapeDtypeStruct((rows, 1), jnp.float32), jax.ShapeDtypeStruct((KV, rows), jnp.bfloat16)]
        + [jax.ShapeDtypeStruct((2, SIDE, HALF, ROWS), jnp.bfloat16)] * 4,
        in_specs=[SMEM, VMEM, VMEM],
        out_specs=[VMEM] * 6,
        scratch_shapes=[pltpu.VMEM((rows, WIDE), jnp.bfloat16)],
        compiler_params=grant(20),
        cost_estimate=pl.CostEstimate(
            flops=rows * width * KV // 2, bytes_accessed=2 * width * (rows + KV // 4), transcendentals=rows
        ),
    )(at, tokens, cotangent)
    return scale, turned, far[:2], far[2:]


def near_kernel(at, turned, x_ref, behind, *refs):
    del behind
    picked = refs[-1]
    depth = x_ref.shape[1] // SIDE
    quarter = x_ref.at[:, pl.ds(pl.multiple_of(pl.program_id(0) * depth, depth), depth)]
    for i, distance in enumerate((0, 1, 3)):
        terms_of(at, turned, quarter, distance, picked, refs[i], refs[3 + i])


def make_near(at, turned, tokens, behind):
    rows, width = tokens.shape
    near = pl.pallas_call(
        near_kernel,
        grid=(SIDE,),
        out_shape=[jax.ShapeDtypeStruct((SIDE, SIDE, HALF, ROWS), jnp.bfloat16)] * 6,
        in_specs=[
            SMEM,
            VMEM,
            VMEM,
            ANY,
        ],
        out_specs=[pl.BlockSpec((1, SIDE, HALF, ROWS), lambda z: (z, 0, 0, 0))] * 6,
        scratch_shapes=[pltpu.VMEM((rows, WIDE), jnp.bfloat16)],
        compiler_params=grant(24),
        cost_estimate=pl.CostEstimate(
            flops=3 * rows * width * KV // 2,
            bytes_accessed=2 * width * (rows + 3 * KV // 4),
            transcendentals=0,
        ),
    )(at, turned, tokens, behind)
    return near[:3], near[3:]


def sum_kernel(at, *refs):
    del at
    out = refs[7]
    for h, terms in enumerate((refs[:3], refs[3:6])):
        for j in range(SIDE):
            value = terms[0][0, j].astype(jnp.float32)
            for term in terms[1:]:
                value = value + term[0, j].astype(jnp.float32)
            out[0, h * SIDE + j] = value.astype(jnp.bfloat16)


def sum_terms(at, terms, behind, first, count):
    level = pl.BlockSpec(
        (1, SIDE, HALF, ROWS), lambda i, at: (at[2 + lax.rem(first + i, SIDE)], 0, 0, 0)
    )
    return pl.pallas_call(
        sum_kernel,
        grid_spec=pltpu.PrefetchScalarGridSpec(
            num_scalar_prefetch=1,
            grid=(count,),
            in_specs=[level] * 6 + [ANY],
            out_specs=pl.BlockSpec((1, 2 * SIDE, HALF, ROWS), lambda i, at: (i, 0, 0, 0)),
        ),
        out_shape=jax.ShapeDtypeStruct((count, 2 * SIDE, HALF, ROWS), jnp.bfloat16),
        compiler_params=grant(12),
        cost_estimate=pl.CostEstimate(flops=0, bytes_accessed=count * 2 * 2**20, transcendentals=0),
    )(at, *terms, behind)


def add_kernel(*refs):
    received, own, out = refs[0], refs[1], refs[-1]
    out[...] = (received[...].astype(jnp.float32) + own[0].astype(jnp.float32)).astype(jnp.bfloat16)


def add_own(received, rest, i, behind=()):
    whole = pl.BlockSpec(received.shape, lambda _: (0, 0, 0))
    return pl.pallas_call(
        add_kernel,
        grid=(1,),
        out_shape=jax.ShapeDtypeStruct(received.shape, received.dtype),
        in_specs=[whole, pl.BlockSpec((1, *received.shape), lambda _: (i, 0, 0, 0))] + [ANY] * len(behind),
        out_specs=whole,
        compiler_params=grant(6),
        cost_estimate=pl.CostEstimate(flops=0, bytes_accessed=2 * 2**20, transcendentals=0),
    )(received, rest, *behind)


def reduce_z(at, terms, behind, last_behind):
    moving = sum_terms(at, terms, behind, 1, 1)[0]
    rest = sum_terms(at, terms, behind, 2, 3)
    moving = add_own(hop_z(moving), rest, 0)
    moving = add_own(hop_z(moving), rest, 1, last_behind)
    return add_own(hop_z(moving), rest, 2)


def project_kernel(at, x_ref, cot_ref, scale_ref, *rest):
    pieces, (values_ref, grad_hbm), (first, second, grad, sems, out_sems) = (rest[:5], rest[5:10]), rest[10:12], rest[12:]
    rows, width = x_ref.shape
    depth = width // SIDE
    copies, blocks = [], []
    for k in range(SIDE):
        z = at[2 + k]
        columns = pl.ds(pl.multiple_of(z * depth, depth), depth)
        blocks.append((z, columns))
        moves = []
        for d in range(SIDE):
            y, x = lax.rem(at[0] + d, SIDE), lax.rem(at[1] + d, SIDE)
            for h in range(2):
                own, after, far_a, far_b, before = pieces[h]
                if d == 2:
                    source = (far_a, far_b)[k // 2].at[k % 2]
                else:
                    source = (own, after, None, before)[d].at[k]
                moves.append((source, first.at[z, y] if h == 0 else second.at[z, :, x]))
        copies.append([pltpu.make_async_copy(a, b, sems.at[k, i]) for i, (a, b) in enumerate(moves)])
        for copy in copies[-1]:
            copy.start()
    scale = scale_ref[...]
    products = [jnp.zeros((rows, HALF), jnp.float32)] * 2
    for k, (z, columns) in enumerate(blocks):
        for copy in copies[k]:
            copy.wait()
        block = x_ref[:, columns]
        products = [
            product + jnp.dot(block, matrix[z].reshape(depth, HALF), preferred_element_type=jnp.float32)
            for product, matrix in zip(products, (first, second))
        ]
    mean = jnp.zeros_like(scale)
    for h, product in enumerate(products):
        columns = slice(h * HALF, (h + 1) * HALF)
        values_ref[:, columns] = (product * scale).astype(jnp.bfloat16)
        mean = mean + jnp.sum(product * cot_ref[:, columns].astype(jnp.float32), axis=-1, keepdims=True)
    slope = scale * scale * scale * (mean / width)
    by_columns = (((1,), (1,)), ((), ()))
    copies = []
    for z in range(SIDE):
        for y in range(SIDE):
            weighted = lax.dot_general(
                cot_ref[:, :HALF], first[z, y].reshape(WIDE, HALF), by_columns, preferred_element_type=jnp.float32
            ) + lax.dot_general(
                cot_ref[:, HALF:], second[z, y].reshape(WIDE, HALF), by_columns, preferred_element_type=jnp.float32
            )
            start = (z * SIDE + y) * WIDE
            columns = slice(start, start + WIDE)
            grad[:, columns] = (scale * weighted - x_ref[:, columns].astype(jnp.float32) * slope).astype(jnp.bfloat16)
        columns = slice(z * depth, (z + 1) * depth)
        copies.append(pltpu.make_async_copy(grad.at[:, columns], grad_hbm.at[:, columns], out_sems.at[z]))
        copies[-1].start()
    for copy in copies:
        copy.wait()


def project(at, tokens, cotangent, scale, pieces):
    rows, width = tokens.shape
    whole = pltpu.VMEM((SIDE, SIDE, SIDE, ROWS, HALF), jnp.bfloat16)
    return pl.pallas_call(
        project_kernel,
        out_shape=[
            jax.ShapeDtypeStruct((rows, KV), jnp.bfloat16),
            jax.ShapeDtypeStruct((rows, width), jnp.bfloat16),
        ],
        in_specs=[SMEM, VMEM, VMEM, VMEM] + [ANY] * 10,
        out_specs=[VMEM, ANY],
        scratch_shapes=[
            whole,
            whole,
            pltpu.VMEM((rows, width), jnp.bfloat16),
            pltpu.SemaphoreType.DMA((SIDE, 8)),
            pltpu.SemaphoreType.DMA((SIDE,)),
        ],
        compiler_params=grant(32),
        cost_estimate=pl.CostEstimate(
            flops=64 * rows * width * KV, bytes_accessed=2 * width * (2 * rows + KV), transcendentals=0
        ),
    )(at, tokens, cotangent, scale, *pieces)


def outer_kernel(fragment_index, assignment, outer, momentum, local, chip, away, outer_out, momentum_out, local_out):
    one, two = find(fragment_index, assignment)
    params, old, mine = outer[...], momentum[...], local[...].astype(jnp.float32)
    summed = chip[...].astype(jnp.float32) + away[...].astype(jnp.float32)
    summed = summed[:2] + summed[2:]
    layer = lax.broadcasted_iota(jnp.int32, params.shape, 0)
    spread = jnp.where(layer == one, summed[0:1], summed[1:2])
    selected = (layer == one) | (layer == two)
    delta = (4.0 * params - spread) / 4.0
    new = nesterov * old + delta
    step = params - outer_rate * (delta + nesterov * new)
    momentum_out[...] = jnp.where(selected, new, old)
    outer_out[...] = jnp.where(selected, step, params)
    local_out[...] = jnp.where(selected, mixing * mine + (1.0 - mixing) * step, mine).astype(jnp.bfloat16)


def outer_step(fragment_index, assignment, outer_params, momentum, local, behind):
    chosen = choose(fragment_index, assignment, local, behind)
    replicas = lax.axis_size("rep")
    chip = jnp.concatenate([chosen, lax.ppermute(chosen, "rep", [(r, r ^ 1) for r in range(replicas)])])
    away = lax.ppermute(chip, "rep", [(r, r ^ 2) for r in range(replicas)])
    return pl.pallas_call(
        outer_kernel,
        out_shape=[
            jax.ShapeDtypeStruct(outer_params.shape, jnp.float32),
            jax.ShapeDtypeStruct(momentum.shape, jnp.float32),
            jax.ShapeDtypeStruct(local.shape, jnp.bfloat16),
        ],
        in_specs=[SMEM, SMEM] + [VMEM] * 5,
        out_specs=[VMEM] * 3,
        compiler_params=grant(8),
    )(fragment_index, assignment, outer_params, momentum, local, chip, away)


def shards(
    tokens,
    cotangent,
    weight,
    norm_gain,
    fragment_index,
    assignment,
    outer_params,
    momentum,
    local_params,
):
    index = lax.axis_index("fsdp")
    z, y, x = index // (SIDE * SIDE), (index // SIDE) % SIDE, index % SIDE
    ring_place = z ^ (z >> 1)
    quarters = [(ring_place - k) & (SIDE - 1) for k in range(SIDE)]
    at = jnp.stack([y, x] + [q ^ (q >> 1) for q in quarters]).astype(jnp.int32)

    row, column = fold(weight[0], norm_gain)
    scale, turned, left_far, right_far = make_far(at, tokens, cotangent)
    cross = gather_small(at, row, column, [turned])
    quarter = [cross]
    for _ in range(SIDE - 1):
        quarter.append(hop_z(quarter[-1]))
    plane, other = split(quarter)

    left, right = make_near(at, turned, tokens, cross)
    terms = reduce_large(left_far, left, 1, quarter[1]) + reduce_large(right_far, right, 2, quarter[1])

    pieces, sent = zip(gather_large(plane, 1), gather_large(other, 2))
    scattered = reduce_z(at, terms, plane, sent)
    values, token_grad = project(at, tokens, cotangent, scale, pieces[0] + pieces[1])

    arrived = reduce_small(scattered[:SIDE], 2, x) + reduce_small(scattered[SIDE:], 1, y)
    weight_grad, gain_grad = finish(at, weight[0], norm_gain, scattered, arrived)

    outer_new, momentum_new, local_new = outer_step(
        fragment_index, assignment, outer_params, momentum, local_params[0], pieces[1][2]
    )
    return (values, token_grad, weight_grad[None], gain_grad, outer_new, momentum_new, local_new[None])


def solution(mesh):
    in_specs = (
        P(("rep", "fsdp"), None),
        P(("rep", "fsdp"), None),
        P("rep", "fsdp", None),
        P("rep", "fsdp"),
        P(),
        P(),
        P(None, "fsdp"),
        P(None, "fsdp"),
        P("rep", None, "fsdp"),
    )
    out_specs = (
        P(("rep", "fsdp"), None),
        P(("rep", "fsdp"), None),
        P("rep", "fsdp", None),
        P("rep", "fsdp"),
        P(None, "fsdp"),
        P(None, "fsdp"),
        P("rep", None, "fsdp"),
    )
    return jax.shard_map(shards, mesh=mesh, in_specs=in_specs, out_specs=out_specs, check_vma=False)
```

```python
import jax
import jax.numpy as jnp
from jax import lax
from jax.experimental import pallas as pl
from jax.experimental.pallas import tpu as pltpu
from jax.sharding import PartitionSpec as P

NFRAG = 4
SIDE = 4
ROWS = 128
KV = 512
HALF = KV // 2
WIDE = SIDE * ROWS
VMEM = pl.BlockSpec(memory_space=pltpu.VMEM)
SMEM = pl.BlockSpec(memory_space=pltpu.SMEM)
ANY = pl.BlockSpec(memory_space=pl.ANY)

epsilon = 1e-05
outer_rate = 0.7
nesterov = 0.9
mixing = 0.5


def grant(mebibytes):
    return pltpu.CompilerParams(vmem_limit_bytes=mebibytes * 2**20)


def flat(z, y, x):
    return (z * SIDE + y) * SIDE + x


def ring(axis, step):
    pairs = []
    for z in range(SIDE):
        for y in range(SIDE):
            for x in range(SIDE):
                to = [z, y, x]
                to[axis] = (to[axis] + step) % SIDE
                pairs.append((flat(z, y, x), flat(*to)))
    return pairs


GRAY = (0, 1, 3, 2)


def z_ring():
    pairs = []
    for place, z in enumerate(GRAY):
        for y in range(SIDE):
            for x in range(SIDE):
                pairs.append((flat(z, y, x), flat(GRAY[(place + 1) % SIDE], y, x)))
    return pairs


def hop_z(value):
    return lax.ppermute(value, "fsdp", z_ring())


def hop(value, axis, step):
    return lax.ppermute(value, "fsdp", ring(axis, step))


def find(fragment_index, assignment):
    current = lax.rem(lax.rem(fragment_index[0], NFRAG) + NFRAG, NFRAG)
    one, two = jnp.int32(-1), jnp.int32(-1)
    for layer in range(assignment.shape[0]):
        chosen = assignment[layer] == current
        two = jnp.where(chosen & (one >= 0), layer, two)
        one = jnp.where(chosen & (one < 0), layer, one)
    return one, two


def choose_kernel(fragment_index, assignment, local, behind, chosen):
    del behind
    value = local[...].astype(jnp.float32)
    layer = lax.broadcasted_iota(jnp.int32, value.shape, 0)
    picks = [
        jnp.sum(jnp.where(layer == which, value, 0.0), axis=0, keepdims=True)
        for which in find(fragment_index, assignment)
    ]
    chosen[...] = jnp.concatenate(picks).astype(jnp.bfloat16)


def choose(fragment_index, assignment, local, behind):
    return pl.pallas_call(
        choose_kernel,
        out_shape=jax.ShapeDtypeStruct((2, local.shape[1]), jnp.bfloat16),
        in_specs=[SMEM, SMEM, VMEM, ANY],
        out_specs=VMEM,
        compiler_params=grant(4),
    )(fragment_index, assignment, local, behind)


def fold_kernel(weight_hbm, gain_hbm, row, column, weight, gain, sems):
    copies = [
        pltpu.make_async_copy(gain_hbm, gain, sems.at[0]),
        pltpu.make_async_copy(weight_hbm, weight, sems.at[1]),
    ]
    for copy in copies:
        copy.start()
    copies[0].wait()
    factor = jnp.broadcast_to(gain[...].astype(jnp.float32), (ROWS, ROWS)).T
    copies[1].wait()
    for j in range(KV // ROWS):
        part = (weight[:, j * ROWS : (j + 1) * ROWS].astype(jnp.float32) * factor).astype(jnp.bfloat16)
        out, at = (row, j * ROWS) if j * ROWS < HALF else (column, j * ROWS - HALF)
        out[:, at : at + ROWS] = part


def fold(weight, gain):
    half = jax.ShapeDtypeStruct((ROWS, HALF), jnp.bfloat16)
    return pl.pallas_call(
        fold_kernel,
        out_shape=[half, half],
        in_specs=[ANY] * 2,
        out_specs=[VMEM] * 2,
        scratch_shapes=[
            pltpu.VMEM(weight.shape, weight.dtype),
            pltpu.VMEM(gain.shape, gain.dtype),
            pltpu.SemaphoreType.DMA((2,)),
        ],
        compiler_params=grant(60),
    )(weight, gain)


def stack_kernel(at, *refs):
    out = refs[-1]
    for d in range(SIDE):
        out[lax.rem(at[1] + d, SIDE)] = refs[d][...]
        out[SIDE + lax.rem(at[0] + d, SIDE)] = refs[SIDE + d][...]


def gather_small(at, row, column, behind):
    parts = [row] + [hop(row, 2, -step) for step in (1, 2, 3)]
    parts += [column] + [hop(column, 1, -step) for step in (1, 2, 3)]
    return pl.pallas_call(
        stack_kernel,
        out_shape=jax.ShapeDtypeStruct((2 * SIDE, ROWS, HALF), jnp.bfloat16),
        in_specs=[SMEM] + [VMEM] * 8 + [ANY] * len(behind),
        out_specs=VMEM,
        compiler_params=grant(4),
    )(at, *parts, *behind)


def split_kernel(*refs):
    left, right = refs[SIDE:]
    for k, part in enumerate(refs[:SIDE]):
        left[k] = part[:SIDE]
        right[k] = part[SIDE:]


def split(parts):
    half = jax.ShapeDtypeStruct((SIDE, SIDE, ROWS, HALF), jnp.bfloat16)
    return pl.pallas_call(
        split_kernel,
        out_shape=[half, half],
        in_specs=[VMEM] * SIDE,
        out_specs=[VMEM] * 2,
        compiler_params=grant(8),
        cost_estimate=pl.CostEstimate(flops=0, bytes_accessed=4 * 2**20, transcendentals=0),
    )(*parts)


def halves_kernel(before, after, far_a, far_b):
    far_a[...] = before[...]
    far_b[...] = after[...]


def gather_large(own, axis):
    before, after = hop(own, axis, 1), hop(own, axis, -1)
    shape = (SIDE // 2, *own.shape[1:])
    half = jax.ShapeDtypeStruct(shape, own.dtype)
    far_a, far_b = pl.pallas_call(
        halves_kernel,
        grid=(1,),
        out_shape=[half, half],
        in_specs=[pl.BlockSpec(shape, lambda i: (0, 0, 0, 0)), pl.BlockSpec(shape, lambda i: (1, 0, 0, 0))],
        out_specs=[pl.BlockSpec(shape, lambda i: (0, 0, 0, 0))] * 2,
        compiler_params=grant(6),
        cost_estimate=pl.CostEstimate(flops=0, bytes_accessed=2 * 2**20, transcendentals=0),
    )(before, after)
    return [own, after, hop(far_a, axis, 1), hop(far_b, axis, -1), before], far_a


def pass_kernel(after, far_a, before, far_b, *rest):
    after_out, before_out = rest[-2:]
    after_out[...] = (after[...].astype(jnp.float32) + far_a[...].astype(jnp.float32)).astype(jnp.bfloat16)
    before_out[...] = (before[...].astype(jnp.float32) + far_b[...].astype(jnp.float32)).astype(jnp.bfloat16)


def pass_on(after, before, far_a, far_b, behind):
    whole = jax.ShapeDtypeStruct(after.shape, after.dtype)
    low = pl.BlockSpec((1, SIDE, HALF, ROWS), lambda z: (z, 0, 0, 0))
    high = pl.BlockSpec((1, SIDE, HALF, ROWS), lambda z: (2 + z, 0, 0, 0))
    return pl.pallas_call(
        pass_kernel,
        grid=(2,),
        out_shape=[whole, whole],
        in_specs=[low, low, high, low, ANY],
        out_specs=[low, high],
        input_output_aliases={0: 0, 2: 1},
        compiler_params=grant(6),
        cost_estimate=pl.CostEstimate(flops=0, bytes_accessed=3 * 2**20, transcendentals=0),
    )(after, far_a, before, far_b, behind)


def reduce_large(far, near, axis, behind):
    own, after, before = near
    after, before = pass_on(after, before, hop(far[0], axis, 1), hop(far[1], axis, -1), behind)
    return [own, hop(after, axis, 1), hop(before, axis, -1)]


def reduce_small(term, axis, place):
    sent = [lax.dynamic_index_in_dim(term, (place + step) % SIDE, 0, False) for step in (1, 2, 3)]
    return [hop(value, axis, step) for step, value in zip((1, 2, 3), sent)]


def finish_kernel(at, weight, gain, scattered, *refs):
    arrived, (weight_grad, gain_grad) = refs[:6], refs[6:]
    row = gain[...].astype(jnp.float32)
    factor = jnp.broadcast_to(row, (ROWS, ROWS)).T
    total = jnp.zeros((1, ROWS), jnp.float32)
    for j in range(KV // ROWS):
        h, low = divmod(j * ROWS, HALF)
        where = at[1] if h == 0 else SIDE + at[0]
        part = scattered[where, low : low + ROWS].astype(jnp.float32)
        for term in arrived[3 * h : 3 * h + 3]:
            part = part + term[low : low + ROWS].astype(jnp.float32)
        columns = slice(j * ROWS, (j + 1) * ROWS)
        weight_grad[:, columns] = part.T * factor
        total = total + jnp.sum(part * weight[:, columns].astype(jnp.float32).T, axis=0, keepdims=True)
    gain_grad[...] = total


def finish(at, weight, gain, scattered, arrived):
    return pl.pallas_call(
        finish_kernel,
        out_shape=[jax.ShapeDtypeStruct((ROWS, KV), jnp.float32), jax.ShapeDtypeStruct((1, ROWS), jnp.float32)],
        in_specs=[SMEM] + [VMEM] * 9,
        out_specs=[VMEM] * 2,
        compiler_params=grant(6),
    )(at, weight, gain, scattered, *arrived)


def columns_of(at, x_ref, distance, picked):
    x = lax.rem(at[1] + distance, SIDE)
    for y in range(SIDE):
        picked[:, y * ROWS : (y + 1) * ROWS] = x_ref[:, pl.ds(pl.multiple_of(y * WIDE + x * ROWS, ROWS), ROWS)]
    return picked[...]


def terms_of(at, turned, x_ref, distance, picked, left, right):
    start = pl.multiple_of(lax.rem(at[0] + distance, SIDE) * WIDE, WIDE)
    for h, columns, out in (
        (0, x_ref[:, pl.ds(start, WIDE)], left),
        (1, columns_of(at, x_ref, distance, picked), right),
    ):
        product = jnp.dot(
            turned[h * HALF : (h + 1) * HALF], columns, preferred_element_type=jnp.float32
        ).astype(jnp.bfloat16)
        for j in range(SIDE):
            out[0, j] = product[:, j * ROWS : (j + 1) * ROWS]


def far_kernel(at, x_ref, cot_ref, scale_ref, turned, left_a, left_b, right_a, right_b, picked):
    rows, width = x_ref.shape
    depth = width // SIDE
    quarters = [slice(z * depth, (z + 1) * depth) for z in range(SIDE)]
    squares = jnp.zeros((rows, ROWS), jnp.float32)
    for j in range(width // ROWS):
        part = x_ref[:, j * ROWS : (j + 1) * ROWS].astype(jnp.float32)
        squares = squares + part * part
    mean = jnp.sum(squares, axis=-1, keepdims=True) / width
    scale = lax.rsqrt(mean + epsilon)
    scale_ref[...] = scale
    turned[...] = (cot_ref[...].astype(jnp.float32) * scale).T.astype(jnp.bfloat16)
    for z in range(SIDE):
        left, right = ((left_a, right_a), (left_b, right_b))[z // 2]
        level = pl.ds(z % 2, 1)
        terms_of(at, turned, x_ref.at[:, quarters[z]], 2, picked, left.at[level], right.at[level])


def make_far(at, tokens, cotangent):
    rows, width = tokens.shape
    scale, turned, *far = pl.pallas_call(
        far_kernel,
        out_shape=[jax.ShapeDtypeStruct((rows, 1), jnp.float32), jax.ShapeDtypeStruct((KV, rows), jnp.bfloat16)]
        + [jax.ShapeDtypeStruct((2, SIDE, HALF, ROWS), jnp.bfloat16)] * 4,
        in_specs=[SMEM, VMEM, VMEM],
        out_specs=[VMEM] * 6,
        scratch_shapes=[pltpu.VMEM((rows, WIDE), jnp.bfloat16)],
        compiler_params=grant(20),
        cost_estimate=pl.CostEstimate(
            flops=rows * width * KV // 2, bytes_accessed=2 * width * (rows + KV // 4), transcendentals=rows
        ),
    )(at, tokens, cotangent)
    return scale, turned, far[:2], far[2:]


def near_kernel(at, turned, x_ref, behind, *refs):
    del behind
    picked = refs[-1]
    depth = x_ref.shape[1] // SIDE
    quarter = x_ref.at[:, pl.ds(pl.multiple_of(pl.program_id(0) * depth, depth), depth)]
    for i, distance in enumerate((0, 1, 3)):
        terms_of(at, turned, quarter, distance, picked, refs[i], refs[3 + i])


def make_near(at, turned, tokens, behind):
    rows, width = tokens.shape
    near = pl.pallas_call(
        near_kernel,
        grid=(SIDE,),
        out_shape=[jax.ShapeDtypeStruct((SIDE, SIDE, HALF, ROWS), jnp.bfloat16)] * 6,
        in_specs=[
            SMEM,
            VMEM,
            VMEM,
            ANY,
        ],
        out_specs=[pl.BlockSpec((1, SIDE, HALF, ROWS), lambda z: (z, 0, 0, 0))] * 6,
        scratch_shapes=[pltpu.VMEM((rows, WIDE), jnp.bfloat16)],
        compiler_params=grant(24),
        cost_estimate=pl.CostEstimate(
            flops=3 * rows * width * KV // 2,
            bytes_accessed=2 * width * (rows + 3 * KV // 4),
            transcendentals=0,
        ),
    )(at, turned, tokens, behind)
    return near[:3], near[3:]


def sum_kernel(at, *refs):
    del at
    out = refs[7]
    for h, terms in enumerate((refs[:3], refs[3:6])):
        for j in range(SIDE):
            value = terms[0][0, j].astype(jnp.float32)
            for term in terms[1:]:
                value = value + term[0, j].astype(jnp.float32)
            out[0, h * SIDE + j] = value.astype(jnp.bfloat16)


def sum_terms(at, terms, behind, first, count):
    level = pl.BlockSpec(
        (1, SIDE, HALF, ROWS), lambda i, at: (at[2 + lax.rem(first + i, SIDE)], 0, 0, 0)
    )
    return pl.pallas_call(
        sum_kernel,
        grid_spec=pltpu.PrefetchScalarGridSpec(
            num_scalar_prefetch=1,
            grid=(count,),
            in_specs=[level] * 6 + [ANY],
            out_specs=pl.BlockSpec((1, 2 * SIDE, HALF, ROWS), lambda i, at: (i, 0, 0, 0)),
        ),
        out_shape=jax.ShapeDtypeStruct((count, 2 * SIDE, HALF, ROWS), jnp.bfloat16),
        compiler_params=grant(12),
        cost_estimate=pl.CostEstimate(flops=0, bytes_accessed=count * 2 * 2**20, transcendentals=0),
    )(at, *terms, behind)


def add_kernel(*refs):
    received, own, out = refs[0], refs[1], refs[-1]
    out[...] = (received[...].astype(jnp.float32) + own[0].astype(jnp.float32)).astype(jnp.bfloat16)


def add_own(received, rest, i, behind=()):
    whole = pl.BlockSpec(received.shape, lambda _: (0, 0, 0))
    return pl.pallas_call(
        add_kernel,
        grid=(1,),
        out_shape=jax.ShapeDtypeStruct(received.shape, received.dtype),
        in_specs=[whole, pl.BlockSpec((1, *received.shape), lambda _: (i, 0, 0, 0))] + [ANY] * len(behind),
        out_specs=whole,
        compiler_params=grant(6),
        cost_estimate=pl.CostEstimate(flops=0, bytes_accessed=2 * 2**20, transcendentals=0),
    )(received, rest, *behind)


def reduce_z(at, terms, behind, last_behind):
    moving = sum_terms(at, terms, behind, 1, 1)[0]
    rest = sum_terms(at, terms, behind, 2, 3)
    moving = add_own(hop_z(moving), rest, 0)
    moving = add_own(hop_z(moving), rest, 1, last_behind)
    return add_own(hop_z(moving), rest, 2)


def project_kernel(at, x_hbm, cot_ref, scale_ref, *rest):
    pieces, (values_ref, grad_hbm), (x_ref, first, second, grad, sems, out_sems) = (rest[:5], rest[5:10]), rest[10:12], rest[12:]
    rows, width = x_ref.shape
    depth = width // SIDE
    copies, blocks = [], []
    for k in range(SIDE):
        z = at[2 + k]
        columns = pl.ds(pl.multiple_of(z * depth, depth), depth)
        blocks.append((z, columns))
        moves = [(x_hbm.at[:, columns], x_ref.at[:, columns])]
        for d in range(SIDE):
            y, x = lax.rem(at[0] + d, SIDE), lax.rem(at[1] + d, SIDE)
            for h in range(2):
                own, after, far_a, far_b, before = pieces[h]
                if d == 2:
                    source = (far_a, far_b)[k // 2].at[k % 2]
                else:
                    source = (own, after, None, before)[d].at[k]
                moves.append((source, first.at[z, y] if h == 0 else second.at[z, :, x]))
        copies.append([pltpu.make_async_copy(a, b, sems.at[k, i]) for i, (a, b) in enumerate(moves)])
        for copy in copies[-1]:
            copy.start()
    scale = scale_ref[...]
    products = [jnp.zeros((rows, HALF), jnp.float32)] * 2
    for k, (z, columns) in enumerate(blocks):
        for copy in copies[k]:
            copy.wait()
        block = x_ref[:, columns]
        products = [
            product + jnp.dot(block, matrix[z].reshape(depth, HALF), preferred_element_type=jnp.float32)
            for product, matrix in zip(products, (first, second))
        ]
    mean = jnp.zeros_like(scale)
    for h, product in enumerate(products):
        columns = slice(h * HALF, (h + 1) * HALF)
        values_ref[:, columns] = (product * scale).astype(jnp.bfloat16)
        mean = mean + jnp.sum(product * cot_ref[:, columns].astype(jnp.float32), axis=-1, keepdims=True)
    slope = scale * scale * scale * (mean / width)
    by_columns = (((1,), (1,)), ((), ()))
    copies = []
    for z in range(SIDE):
        for y in range(SIDE):
            weighted = lax.dot_general(
                cot_ref[:, :HALF], first[z, y].reshape(WIDE, HALF), by_columns, preferred_element_type=jnp.float32
            ) + lax.dot_general(
                cot_ref[:, HALF:], second[z, y].reshape(WIDE, HALF), by_columns, preferred_element_type=jnp.float32
            )
            start = (z * SIDE + y) * WIDE
            columns = slice(start, start + WIDE)
            grad[:, columns] = (scale * weighted - x_ref[:, columns].astype(jnp.float32) * slope).astype(jnp.bfloat16)
        columns = slice(z * depth, (z + 1) * depth)
        copies.append(pltpu.make_async_copy(grad.at[:, columns], grad_hbm.at[:, columns], out_sems.at[z]))
        copies[-1].start()
    for copy in copies:
        copy.wait()


def project(at, tokens, cotangent, scale, pieces):
    rows, width = tokens.shape
    whole = pltpu.VMEM((SIDE, SIDE, SIDE, ROWS, HALF), jnp.bfloat16)
    return pl.pallas_call(
        project_kernel,
        out_shape=[
            jax.ShapeDtypeStruct((rows, KV), jnp.bfloat16),
            jax.ShapeDtypeStruct((rows, width), jnp.bfloat16),
        ],
        in_specs=[SMEM, ANY, VMEM, VMEM] + [ANY] * 10,
        out_specs=[VMEM, ANY],
        scratch_shapes=[
            pltpu.VMEM((rows, width), jnp.bfloat16),
            whole,
            whole,
            pltpu.VMEM((rows, width), jnp.bfloat16),
            pltpu.SemaphoreType.DMA((SIDE, 9)),
            pltpu.SemaphoreType.DMA((SIDE,)),
        ],
        compiler_params=grant(53),
        cost_estimate=pl.CostEstimate(
            flops=64 * rows * width * KV, bytes_accessed=2 * width * (2 * rows + KV), transcendentals=0
        ),
    )(at, tokens, cotangent, scale, *pieces)


def outer_kernel(fragment_index, assignment, outer, momentum, local, chip, away, outer_out, momentum_out, local_out):
    one, two = find(fragment_index, assignment)
    params, old, mine = outer[...], momentum[...], local[...].astype(jnp.float32)
    summed = chip[...].astype(jnp.float32) + away[...].astype(jnp.float32)
    summed = summed[:2] + summed[2:]
    layer = lax.broadcasted_iota(jnp.int32, params.shape, 0)
    spread = jnp.where(layer == one, summed[0:1], summed[1:2])
    selected = (layer == one) | (layer == two)
    delta = (4.0 * params - spread) / 4.0
    new = nesterov * old + delta
    step = params - outer_rate * (delta + nesterov * new)
    momentum_out[...] = jnp.where(selected, new, old)
    outer_out[...] = jnp.where(selected, step, params)
    local_out[...] = jnp.where(selected, mixing * mine + (1.0 - mixing) * step, mine).astype(jnp.bfloat16)


def outer_step(fragment_index, assignment, outer_params, momentum, local, behind):
    chosen = choose(fragment_index, assignment, local, behind)
    replicas = lax.axis_size("rep")
    chip = jnp.concatenate([chosen, lax.ppermute(chosen, "rep", [(r, r ^ 1) for r in range(replicas)])])
    away = lax.ppermute(chip, "rep", [(r, r ^ 2) for r in range(replicas)])
    return pl.pallas_call(
        outer_kernel,
        out_shape=[
            jax.ShapeDtypeStruct(outer_params.shape, jnp.float32),
            jax.ShapeDtypeStruct(momentum.shape, jnp.float32),
            jax.ShapeDtypeStruct(local.shape, jnp.bfloat16),
        ],
        in_specs=[SMEM, SMEM] + [VMEM] * 5,
        out_specs=[VMEM] * 3,
        compiler_params=grant(8),
    )(fragment_index, assignment, outer_params, momentum, local, chip, away)


def shards(
    tokens,
    cotangent,
    weight,
    norm_gain,
    fragment_index,
    assignment,
    outer_params,
    momentum,
    local_params,
):
    index = lax.axis_index("fsdp")
    z, y, x = index // (SIDE * SIDE), (index // SIDE) % SIDE, index % SIDE
    ring_place = z ^ (z >> 1)
    quarters = [(ring_place - k) & (SIDE - 1) for k in range(SIDE)]
    at = jnp.stack([y, x] + [q ^ (q >> 1) for q in quarters]).astype(jnp.int32)

    row, column = fold(weight[0], norm_gain)
    scale, turned, left_far, right_far = make_far(at, tokens, cotangent)
    cross = gather_small(at, row, column, [turned])
    quarter = [cross]
    for _ in range(SIDE - 1):
        quarter.append(hop_z(quarter[-1]))
    plane, other = split(quarter)

    left, right = make_near(at, turned, tokens, cross)
    terms = reduce_large(left_far, left, 1, quarter[1]) + reduce_large(right_far, right, 2, quarter[1])

    pieces, sent = zip(gather_large(plane, 1), gather_large(other, 2))
    scattered = reduce_z(at, terms, plane, sent)
    values, token_grad = project(at, tokens, cotangent, scale, pieces[0] + pieces[1])

    arrived = reduce_small(scattered[:SIDE], 2, x) + reduce_small(scattered[SIDE:], 1, y)
    weight_grad, gain_grad = finish(at, weight[0], norm_gain, scattered, arrived)

    outer_new, momentum_new, local_new = outer_step(
        fragment_index, assignment, outer_params, momentum, local_params[0], pieces[1][2]
    )
    return (values, token_grad, weight_grad[None], gain_grad, outer_new, momentum_new, local_new[None])


def solution(mesh):
    in_specs = (
        P(("rep", "fsdp"), None),
        P(("rep", "fsdp"), None),
        P("rep", "fsdp", None),
        P("rep", "fsdp"),
        P(),
        P(),
        P(None, "fsdp"),
        P(None, "fsdp"),
        P("rep", None, "fsdp"),
    )
    out_specs = (
        P(("rep", "fsdp"), None),
        P(("rep", "fsdp"), None),
        P("rep", "fsdp", None),
        P("rep", "fsdp"),
        P(None, "fsdp"),
        P(None, "fsdp"),
        P("rep", None, "fsdp"),
    )
    return jax.shard_map(shards, mesh=mesh, in_specs=in_specs, out_specs=out_specs, check_vma=False)
```
